128 devices in a mesh: dp: 16 (over y, x_lo, core), group: 8 (over z, x_hi).
Axes of the slice: x: 4 (x_hi: 2, x_lo: 2; x = x_hi * 2 + x_lo), y: 4, z: 4, core: 2. Of those that a mesh axis runs over, the one named last changes fastest.
Arguments:
- tokens: bfloat16 [65536, 4096], P('dp', 'group'), may hold values from -6 to 6
- router_weight: float32 [4096, 256], P('group'), may hold values from -1 to 1
- gate_weight: bfloat16 [8, 4096, 8192], P('group', None, 'dp'), may hold values from -0.09375 to 0.09375
- up_weight: bfloat16 [8, 4096, 8192], P('group', None, 'dp'), may hold values from -0.09375 to 0.09375
- down_weight: bfloat16 [8, 8192, 4096], P('group', 'dp'), may hold values from -2 to 2
- picks: int32 [8, 512], replicated, may hold values from 0 to 65535, as said below
Outputs:
- mixed: bfloat16 [65536, 4096], P('dp', 'group')
The draws below stay inside these ranges and needn't reach their ends.
Inputs may be any that keep to these rules, and one draw needn't show every extreme that they name: picks holds token indices of 0 to 65535; a token may stand in several slots.
All inputs are finite; a program needn't handle non-finite values.
Results may differ from the reference program's by a relative error of at most 0.013.
Values may be sent and summed in bfloat16 or wider, within the bound.
A program may use at most 128 MiB of HBM per device.

```python
import jax
import jax.numpy as jnp
from jax import lax

D = 4096
FF = 8192
EXP_GRP = 32
EXP_FLY = 1
TOKENS = 65536
EXPERTS = 256
FLIGHT = 8
CAP = 512


def special_rows(key):
    rows = jax.random.randint(jax.random.fold_in(key, 77), (3,), 0, TOKENS)
    values = jnp.clip(jax.random.normal(jax.random.fold_in(key, 78), (3, D), jnp.float32), -6.0, 6.0)
    return (rows, values)


def computed_scale():
    column_ids = jnp.arange(EXPERTS, dtype=jnp.int32)
    return jnp.where(column_ids % EXP_GRP < EXP_FLY, 1.0 / 30.0, 1.0).astype(jnp.float32)


def draw_tokens(key, part):
    rows, values = special_rows(key)
    key = jax.random.fold_in(key, 1)
    base = jnp.clip(jax.random.normal(key, (TOKENS, D), jnp.float32), -6.0, 6.0)
    base = base.at[rows].set(values)
    return base.astype(jnp.bfloat16)


def draw_router_weight(key, part):
    key = jax.random.fold_in(key, 2)
    base = jnp.clip(jax.random.normal(key, (D, EXPERTS), jnp.float32), -6.0, 6.0) * (3.0 / D ** 0.5)
    base = base * computed_scale()[None, :]
    return base


def draw_picks(key, part):
    rows, values = special_rows(key)
    key = jax.random.fold_in(key, 3)
    base = jax.random.randint(key, (FLIGHT, CAP), 0, TOKENS).astype(jnp.int32)
    head = jnp.concatenate([jnp.array([0, TOKENS - 1], jnp.int32), rows.astype(jnp.int32)])
    return base.at[0, :5].set(head)


def levels(key, extent, cuts, smallest, largest):
    loudness, own = 1.0, jax.random.fold_in(key, 6)
    for dim, shards_of in cuts:
        heights = jnp.exp(jax.random.uniform(jax.random.fold_in(own, dim), (shards_of,), jnp.float32, smallest / len(cuts), largest / len(cuts)))
        loudness = loudness * jnp.repeat(heights, extent[dim] // shards_of).reshape([-1 if axis == dim else 1 for axis in range(len(extent))])
    return loudness


def scatter_about(key, extent, scale, most, pieces=(), held_as=jnp.bfloat16):
    values = scale * jax.random.normal(key, extent, jnp.float32)
    if pieces:
        values = values * levels(key, extent, pieces, -0.22, 0.18)
    return jnp.clip(values, -most, most).astype(held_as)


def setup_inputs(seed: int = 0) -> dict:
    seeds = jax.random.split(jax.random.key(seed), 7)
    return {
        "tokens": draw_tokens(jax.random.fold_in(seeds[6], 71), 0),
        "router_weight": draw_router_weight(jax.random.fold_in(seeds[6], 71), 0),
        "gate_weight": scatter_about(seeds[2], (FLIGHT, D, FF), D ** -0.5, 0.09375, ((0, 8), (2, 16))),
        "up_weight": scatter_about(seeds[3], (FLIGHT, D, FF), D ** -0.5, 0.09375, ((0, 8), (2, 16))),
        "down_weight": scatter_about(seeds[4], (FLIGHT, FF, D), (max(FF // 1024, 1)) ** -0.5, 2.0, ((0, 8), (1, 16))),
        "picks": draw_picks(jax.random.fold_in(seeds[6], 71), 0),
    }


def reference(tokens, router_weight, gate_weight, up_weight, down_weight, picks):
    logits = jnp.dot(tokens.astype(jnp.float32), router_weight, preferred_element_type=jnp.float32)
    probs = jax.nn.softmax(logits, axis=-1)
    slot_ids = jnp.arange(FLIGHT, dtype=jnp.int32)
    columns = (slot_ids // EXP_FLY) * EXP_GRP + slot_ids % EXP_FLY

    def expert(packed):
        row_index, column, w_gate, w_up, w_down = packed
        rows = jnp.take(tokens, row_index, axis=0)
        gate_h = jnp.dot(rows, w_gate, preferred_element_type=jnp.float32)
        up_h = jnp.dot(rows, w_up, preferred_element_type=jnp.float32)
        hidden = (jax.nn.silu(gate_h) * up_h).astype(jnp.bfloat16)
        expert_out = jnp.dot(hidden, w_down, preferred_element_type=jnp.float32).astype(jnp.bfloat16)
        gates = probs[row_index, column]
        return (gates[:, None] * expert_out.astype(jnp.float32)).astype(jnp.bfloat16)

    weighted = lax.map(expert, (picks, columns, gate_weight, up_weight, down_weight))
    mixed = jnp.zeros((TOKENS, D), jnp.float32)
    mixed = mixed.at[picks.reshape(-1)].add(weighted.reshape(-1, D).astype(jnp.float32))
    return mixed.astype(jnp.bfloat16)
```

```python
import functools

import jax
import jax.numpy as jnp
from jax import lax
from jax.experimental import pallas as pl
from jax.experimental.pallas import tpu as pltpu
from jax.sharding import PartitionSpec as P

MESH = pl.DeviceIdType.MESH
BF16 = jnp.bfloat16
F32 = jnp.float32
DP = 16
GRP = 8
CAPS = (48, 256)
BLK = 256
ROWS = 32
HALF = 16


def iota(shape, dim, dtype=jnp.int32):
    out = lax.broadcasted_iota(jnp.int32, shape, dim)
    return out if dtype == jnp.int32 else out.astype(dtype)


def earlier(n):
    return jnp.where(iota((n, n), 0) < iota((n, n), 1), 1.0, 0.0).astype(BF16)


def expert_kernel(
    picks_ref, tok_hbm, wr_hbm, wg_hbm, wu_hbm, wd_hbm,
    back_ref, index_ref,
    tok, wr, wg, wu, wd, onehot, packed, arrived, spread, rows, logit_part, logit_all,
    x, hidden, part, core_in, h0_in, h1_in, h1_edge, weighted, returned, outgoing,
    load_sem, own_sem,
    tok_ss, tok_rs, row_ss, row_rs, log_ss, log_rs, ag_ss, ag_rs, sib_ss, sib_rs,
    core_ss, core_rs, rs_ss, rs_rs, ret_ss, ret_rs, out_ss, out_rs,
):
    cap = packed.shape[1]
    step_blocks = onehot.shape[0] // cap
    d, g = lax.axis_index("dp"), lax.axis_index("group")
    y, xl, core = d // 4, (d // 2) % 2, d % 2
    tok_rows = tok.shape[0]
    feats = tok.shape[1]

    def block(yy, xx, cc):
        return (yy * 2 + xx) * 2 + cc

    up, down, far = (y + 1) % 4, (y + 3) % 4, (y + 2) % 4
    ox, oc = 1 - xl, 1 - core
    to_up = (block(up, xl, core), g)
    to_down = (block(down, xl, core), g)
    to_x = (block(y, ox, core), g)
    to_core = (block(y, xl, oc), g)

    sent = []

    def remote(src, dst, ss, rs, device):
        return pltpu.make_async_remote_copy(
            src_ref=src, dst_ref=dst, send_sem=ss, recv_sem=rs, device_id=device, device_id_type=MESH
        )

    def send(src, dst, ss, rs, device):
        copy = remote(src, dst, ss, rs, device)
        copy.start()
        sent.append(copy)
        return copy

    loads = []
    for i, (src, dst) in enumerate(
        ((tok_hbm, tok), (wr_hbm, wr), (wg_hbm, wg), (wu_hbm, wu), (wd_hbm, wd))
    ):
        copy = pltpu.make_async_copy(src, dst, load_sem.at[i])
        copy.start()
        loads.append(copy)

    barrier = pltpu.get_barrier_semaphore()
    for k in range(1, DP):
        pl.semaphore_signal(barrier, inc=1, device_id=((d + k) % DP, g), device_id_type=MESH)
    for k in range(1, GRP):
        pl.semaphore_signal(barrier, inc=1, device_id=(d, (g + k) % GRP), device_id_type=MESH)

    tri = earlier(BLK)
    local = picks_ref[...] - d * tok_rows
    mine = (local >= 0) & (local < tok_rows)
    rank = jnp.dot(
        jnp.where(mine, 1.0, 0.0).astype(BF16), tri, preferred_element_type=F32
    )
    rank = jnp.where(mine, rank, -1.0)
    local = local.astype(F32)
    slot_rank = iota((cap, BLK), 0, F32)
    for b in range(DP):
        chosen = jnp.where(slot_rank == rank[b : b + 1, :], local[b : b + 1, :], -1.0)
        index = jnp.max(chosen, axis=1, keepdims=True)
        index_ref[pl.ds(b * cap, cap), :] = jnp.broadcast_to(index, (cap, 128))

    owner = picks_ref[pl.ds(d, 1), :] // tok_rows
    is_owner = jnp.where(iota((DP, BLK), 0) == owner, 1.0, 0.0)
    ranks = jnp.dot(is_owner.astype(BF16), tri, preferred_element_type=F32)
    place = jnp.sum(is_owner * ranks, axis=0, keepdims=True) + owner.astype(F32) * cap
    spread[...] = jnp.where(iota((DP * cap, BLK), 0, F32) == place, 1.0, 0.0).astype(BF16)

    loads[0].wait()
    pl.semaphore_wait(barrier, DP - 1 + GRP - 1)
    lanes = iota((step_blocks * cap, 128), 1, F32)

    def gather(step, carry):
        turn = step * step_blocks // 4
        yy = (y + jnp.where(turn == 2, 3, jnp.where(turn == 3, 0, 2 - turn))) % 4
        first = yy * 4 + step * step_blocks % 4
        index = index_ref[pl.ds(pl.multiple_of(first * cap, 16), step_blocks * cap), :]
        for t in range(tok_rows // 128):
            onehot[:, t * 128 : (t + 1) * 128] = jnp.where(
                index == lanes + float(t * 128), 1.0, 0.0
            ).astype(BF16)
        taken = jnp.dot(onehot[...], tok[...], preferred_element_type=F32).astype(BF16)
        packed[pl.ds(first, step_blocks)] = taken.reshape(step_blocks, cap, feats)
        for i in range(step_blocks):
            to = first + i
            k = (to - d + DP) % DP

            @pl.when(to != d)
            def _():
                remote(packed.at[to], arrived.at[d], tok_ss.at[k], tok_rs.at[k], (to, g)).start()

        return carry

    lax.fori_loop(0, DP // step_blocks, gather, 0)
    own = pltpu.make_async_copy(packed.at[d], arrived.at[d], own_sem.at[0])
    own.start()
    loads[1].wait()
    hi = wr[...].astype(BF16)
    lo = (wr[...] - hi.astype(F32)).astype(BF16)
    own.wait()
    for k in range(1, DP):
        frm = (d - k + DP) % DP
        remote(packed.at[frm], arrived.at[frm], tok_ss.at[k], tok_rs.at[k], (frm, g)).wait_recv()

    taken = lax.dot_general(
        spread[...], arrived[...].reshape(DP * cap, feats), (((0,), (0,)), ((), ())),
        preferred_element_type=F32,
    ).astype(BF16)
    rows[...] = taken.reshape(GRP, ROWS, feats)
    mine_cols = pl.ds(pl.multiple_of(g * feats, feats), feats)
    for k in range(1, GRP):
        q = (g + k) % GRP
        send(rows.at[q], x.at[d, :, mine_cols], row_ss.at[k], row_rs.at[k], (d, q))
    own = pltpu.make_async_copy(rows.at[g], x.at[d, :, mine_cols], own_sem.at[1])
    own.start()
    logits = jnp.dot(taken, hi, preferred_element_type=F32) + jnp.dot(
        taken, lo, preferred_element_type=F32
    )
    logit_part[...] = logits.reshape(GRP, ROWS, logits.shape[1])
    own.wait()
    for k in range(1, GRP):
        frm = (g - k + GRP) % GRP
        cols = pl.ds(pl.multiple_of(frm * feats, feats), feats)
        remote(rows.at[frm], x.at[d, :, cols], row_ss.at[k], row_rs.at[k], (d, frm)).wait_recv()

    h0, h1 = pl.ds(0, HALF), pl.ds(HALF, HALF)
    wide = x.shape[2]
    left, right = pl.ds(0, wide // 2), pl.ds(wide // 2, wide // 2)

    def ag(i, b, half, to, cols=None):
        ref = x.at[b, half] if cols is None else x.at[b, half, cols]
        return send(ref, ref, ag_ss.at[i], ag_rs.at[i], to)

    def got(i, b, half, cols=None):
        ref = x.at[b, half] if cols is None else x.at[b, half, cols]
        remote(ref, ref, ag_ss.at[i], ag_rs.at[i], to_x).wait_recv()

    n_sib = [0]

    def sib(b, half):
        ref = x.at[b, half]
        send(ref, ref, sib_ss.at[n_sib[0]], sib_rs.at[n_sib[0]], to_core)
        n_sib[0] += 1

    own_b, x_b = block(y, xl, core), block(y, ox, core)
    up_b, down_b, far_b = block(up, xl, core), block(down, xl, core), block(far, xl, core)
    up_x, down_x, far_x = block(up, ox, core), block(down, ox, core), block(far, ox, core)
    ag(0, own_b, h0, to_x)
    ag(7, own_b, h1, to_up)
    ag(8, own_b, h1, to_down)
    ag(1, own_b, h0, to_up)
    ag(2, own_b, h0, to_down)
    ag(9, own_b, h1, to_x)
    sib(own_b, h0)
    sib(own_b, h1)
    for k in range(1, GRP):
        q = (g + k) % GRP
        send(logit_part.at[q], logit_all.at[g], log_ss.at[k], log_rs.at[k], (d, q))
    own2 = pltpu.make_async_copy(logit_part.at[g], logit_all.at[g], own_sem.at[2])
    own2.start()
    got(0, x_b, h0)
    ag(3, x_b, h0, to_up)
    ag(4, x_b, h0, to_down)
    sib(x_b, h0)
    got(7, down_b, h1)
    ag(10, down_b, h1, to_up, left)
    ag(12, down_b, h1, to_x)
    sib(down_b, h1)
    got(8, up_b, h1)
    ag(11, up_b, h1, to_down, right)
    ag(13, up_b, h1, to_x)
    sib(up_b, h1)
    got(1, down_b, h0)
    ag(5, down_b, h0, to_up)
    sib(down_b, h0)
    got(2, up_b, h0)
    sib(up_b, h0)
    got(9, x_b, h1)
    sib(x_b, h1)
    got(4, up_x, h0)
    ag(6, up_x, h0, to_down)
    sib(up_x, h0)
    got(3, down_x, h0)
    sib(down_x, h0)
    got(10, far_b, h1, left)
    got(11, far_b, h1, right)
    ag(14, far_b, h1, to_x)
    sib(far_b, h1)
    got(12, down_x, h1)
    sib(down_x, h1)
    got(13, up_x, h1)
    sib(up_x, h1)
    got(5, far_b, h0)
    sib(far_b, h0)
    got(6, far_x, h0)
    sib(far_x, h0)
    got(14, far_x, h1)
    sib(far_x, h1)
    n_sib[0] = 0
    for i in range(16):
        ref = x.at[block(y, xl, oc), h0]
        remote(ref, ref, sib_ss.at[i], sib_rs.at[i], to_core).wait_recv()

    loads[2].wait()
    loads[3].wait()
    n_rows = DP * ROWS
    units = wg.shape[1]

    def into_hidden(step, carry):
        m = step // 2
        cols = pl.ds(pl.multiple_of((step % 2) * (units // 2), 128), units // 2)
        xs = x[pl.ds(m * 8, 8)].reshape(n_rows // 2, wide)
        gate = jnp.dot(xs, wg[:, cols], preferred_element_type=F32)
        lift = jnp.dot(xs, wu[:, cols], preferred_element_type=F32)
        value = gate / (1.0 + jnp.exp(-gate)) * lift
        hidden[pl.ds(pl.multiple_of(m * (n_rows // 2), 16), n_rows // 2), cols] = value.astype(BF16)
        return carry

    lax.fori_loop(0, 4, into_hidden, 0)
    loads[4].wait()

    def out_of_hidden(yy):
        hs = hidden[pl.ds(pl.multiple_of(yy * 4 * ROWS, 16), 4 * ROWS), :]

        def tile(step, carry):
            cols = pl.ds(pl.multiple_of(step * 512, 512), 512)
            value = jnp.dot(hs, wd[:, cols], preferred_element_type=F32).astype(BF16)
            part[pl.ds(yy * 4, 4), :, cols] = value.reshape(4, ROWS, 512)
            return carry

        lax.fori_loop(0, wide // 512, tile, 0)

    def to_sibling(i, yy):
        for xx in range(2):
            send(
                part.at[block(yy, xx, oc)], core_in.at[yy * 2 + xx],
                core_ss.at[2 * i + xx], core_rs.at[2 * i + xx], to_core,
            )

    def add_sibling(i, yy):
        for xx in range(2):
            b = block(yy, xx, core)
            remote(
                part.at[b], core_in.at[yy * 2 + xx],
                core_ss.at[2 * i + xx], core_rs.at[2 * i + xx], to_core,
            ).wait_recv()
            part[b] = (part[b].astype(F32) + core_in[yy * 2 + xx].astype(F32)).astype(BF16)

    def rs(i, src, dst, to):
        send(src, dst, rs_ss.at[i], rs_rs.at[i], to)

    def rs_got(i, dst):
        remote(dst, dst, rs_ss.at[i], rs_rs.at[i], to_x).wait_recv()

    def add(b, half, ref, cols=None):
        if cols is None:
            part[b, half] = (part[b, half].astype(F32) + ref[...].astype(F32)).astype(BF16)
        else:
            part[b, half, cols] = (part[b, half, cols].astype(F32) + ref[...].astype(F32)).astype(BF16)

    out_of_hidden(far)
    to_sibling(0, far)
    out_of_hidden(up)
    to_sibling(1, up)
    add_sibling(0, far)
    rs(0, part.at[far_b, h0], h0_in.at[0], to_up)
    rs(1, part.at[far_x, h0], h0_in.at[1], to_down)
    rs(7, part.at[far_x, h1], h1_in.at[0], to_x)
    out_of_hidden(down)
    to_sibling(2, down)
    add_sibling(1, up)
    rs(2, part.at[up_x, h0], h0_in.at[2], to_up)
    rs(8, part.at[up_x, h1], h1_in.at[1], to_x)
    rs_got(7, h1_in.at[0])
    add(far_b, h1, h1_in.at[0])
    rs(9, part.at[far_b, h1, left], h1_edge.at[0], to_up)
    rs(10, part.at[far_b, h1, right], h1_edge.at[1], to_down)
    out_of_hidden(y)
    to_sibling(3, y)
    add_sibling(2, down)
    rs(3, part.at[down_b, h0], h0_in.at[3], to_down)
    rs(11, part.at[down_x, h1], h1_in.at[2], to_x)
    rs_got(0, h0_in.at[0])
    add(up_b, h0, h0_in.at[0])
    rs(4, part.at[up_b, h0], h0_in.at[4], to_up)
    rs_got(1, h0_in.at[1])
    add(down_x, h0, h0_in.at[1])
    rs(5, part.at[down_x, h0], h0_in.at[5], to_down)
    rs_got(8, h1_in.at[1])
    add(up_b, h1, h1_in.at[1])
    rs_got(9, h1_edge.at[0])
    add(up_b, h1, h1_edge.at[0], left)
    rs(12, part.at[up_b, h1], h1_in.at[4], to_up)
    rs_got(11, h1_in.at[2])
    add(down_b, h1, h1_in.at[2])
    rs_got(10, h1_edge.at[1])
    add(down_b, h1, h1_edge.at[1], right)
    rs(13, part.at[down_b, h1], h1_in.at[5], to_down)
    add_sibling(3, y)
    rs(14, part.at[x_b, h1], h1_in.at[3], to_x)

    own2.wait()
    for k in range(1, GRP):
        frm = (g - k + GRP) % GRP
        remote(logit_part.at[frm], logit_all.at[frm], log_ss.at[k], log_rs.at[k], (d, frm)).wait_recv()
    logits = logit_all[0]
    for q in range(1, GRP):
        logits = logits + logit_all[q]
    n_exp = logits.shape[1]
    grown = jnp.exp(logits - jnp.max(logits, axis=1, keepdims=True))
    column = iota(logits.shape, 1) == g * (n_exp // GRP)
    prob = jnp.sum(jnp.where(column, grown, 0.0), axis=1, keepdims=True) / jnp.sum(
        grown, axis=1, keepdims=True
    )

    rs_got(2, h0_in.at[2])
    rs_got(5, h0_in.at[5])
    part[x_b, h0] = (
        part[x_b, h0].astype(F32) + h0_in[2].astype(F32) + h0_in[5].astype(F32)
    ).astype(BF16)
    rs(6, part.at[x_b, h0], h0_in.at[6], to_x)
    rs_got(3, h0_in.at[3])
    rs_got(4, h0_in.at[4])
    first = part[own_b, h0].astype(F32) + h0_in[3].astype(F32) + h0_in[4].astype(F32)
    rs_got(6, h0_in.at[6])
    first = (first + h0_in[6].astype(F32)).astype(BF16).astype(F32)
    weighted[h0] = (first * prob[:HALF]).astype(BF16)
    rs_got(14, h1_in.at[3])
    rs_got(12, h1_in.at[4])
    rs_got(13, h1_in.at[5])
    second = part[own_b, h1].astype(F32) + h1_in[3].astype(F32)
    second = second + h1_in[4].astype(F32) + h1_in[5].astype(F32)
    weighted[h1] = (second.astype(BF16).astype(F32) * prob[HALF:]).astype(BF16)

    for k in range(1, GRP):
        q = (g + k) % GRP
        cols = pl.ds(pl.multiple_of(q * feats, feats), feats)
        send(weighted.at[:, cols], returned.at[g], ret_ss.at[k], ret_rs.at[k], (d, q))
    own = pltpu.make_async_copy(weighted.at[:, mine_cols], returned.at[g], own_sem.at[3])
    own.start()
    own.wait()
    for k in range(1, GRP):
        frm = (g - k + GRP) % GRP
        remote(returned.at[frm], returned.at[frm], ret_ss.at[k], ret_rs.at[k], (d, frm)).wait_recv()

    back = jnp.dot(
        spread[...], returned[...].reshape(BLK, feats), preferred_element_type=F32
    ).astype(BF16)
    outgoing[...] = back.reshape(DP, cap, feats)
    for k in range(1, DP):
        to = (d + k) % DP
        send(outgoing.at[to], back_ref.at[d], out_ss.at[k], out_rs.at[k], (to, g))
    own = pltpu.make_async_copy(outgoing.at[d], back_ref.at[d], own_sem.at[4])
    own.start()
    own.wait()
    for k in range(1, DP):
        frm = (d - k + DP) % DP
        remote(outgoing.at[frm], back_ref.at[frm], out_ss.at[k], out_rs.at[k], (frm, g)).wait_recv()

    for k in range(1, DP):
        to = (d + k) % DP
        remote(packed.at[to], arrived.at[d], tok_ss.at[k], tok_rs.at[k], (to, g)).wait_send()
    for copy in sent:
        copy.wait_send()


def mix_kernel(index_ref, back_ref, out_ref, index_rows):
    tile = out_ref.shape[0]
    packed = index_ref.shape[0]

    @pl.when(pl.program_id(0) == 0)
    def _():
        index_rows[...] = index_ref[...].T

    first = (pl.program_id(0) * tile).astype(F32)
    parts = []
    for t in range(tile // 128):
        token = iota((128, packed), 0, F32) + (first + float(t * 128))
        parts.append(jnp.where(index_rows[...] == token, 1.0, 0.0).astype(BF16))
    onehot = jnp.concatenate(parts, axis=0)
    out_ref[...] = jnp.dot(onehot, back_ref[...], preferred_element_type=F32).astype(BF16)


def kernel_shards(tokens, router_weight, gate_weight, up_weight, down_weight, blocks, cap):
    packed = DP * cap
    step_rows = 4 * cap if cap < 64 else cap
    tok_rows, feats = tokens.shape
    units, wide = down_weight.shape[1:]
    n_exp = router_weight.shape[1]
    dma = pltpu.SemaphoreType.DMA
    any_spec = pl.BlockSpec(memory_space=pl.ANY)
    vmem_spec = pl.BlockSpec(memory_space=pltpu.VMEM)
    back, index = pl.pallas_call(
        expert_kernel,
        out_shape=(
            jax.ShapeDtypeStruct((DP, cap, feats), BF16),
            jax.ShapeDtypeStruct((packed, 128), F32),
        ),
        in_specs=[vmem_spec] + [any_spec] * 5,
        out_specs=(any_spec, vmem_spec),
        scratch_shapes=[
            pltpu.VMEM((tok_rows, feats), BF16),
            pltpu.VMEM((feats, n_exp), F32),
            pltpu.VMEM((wide, units), BF16),
            pltpu.VMEM((wide, units), BF16),
            pltpu.VMEM((units, wide), BF16),
            pltpu.VMEM((step_rows, tok_rows), BF16),
            pltpu.VMEM((DP, cap, feats), BF16),
            pltpu.VMEM((DP, cap, feats), BF16),
            pltpu.VMEM((packed, BLK), BF16),
            pltpu.VMEM((GRP, ROWS, feats), BF16),
            pltpu.VMEM((GRP, ROWS, n_exp), F32),
            pltpu.VMEM((GRP, ROWS, n_exp), F32),
            pltpu.VMEM((DP, ROWS, wide), BF16),
            pltpu.VMEM((DP * ROWS, units), BF16),
            pltpu.VMEM((DP, ROWS, wide), BF16),
            pltpu.VMEM((DP // 2, ROWS, wide), BF16),
            pltpu.VMEM((7, HALF, wide), BF16),
            pltpu.VMEM((6, HALF, wide), BF16),
            pltpu.VMEM((2, HALF, wide // 2), BF16),
            pltpu.VMEM((ROWS, wide), BF16),
            pltpu.VMEM((GRP, ROWS, feats), BF16),
            pltpu.VMEM((DP, cap, feats), BF16),
            dma((5,)),
            dma((5,)),
            dma((DP,)), dma((DP,)),
            dma((GRP,)), dma((GRP,)),
            dma((GRP,)), dma((GRP,)),
            dma((15,)), dma((15,)),
            dma((16,)), dma((16,)),
            dma((8,)), dma((8,)),
            dma((15,)), dma((15,)),
            dma((GRP,)), dma((GRP,)),
            dma((DP,)), dma((DP,)),
        ],
        compiler_params=pltpu.CompilerParams(
            collective_id=cap, has_side_effects=True, vmem_limit_bytes=60 * 2**20
        ),
        cost_estimate=pl.CostEstimate(
            flops=11 * 10**9, bytes_accessed=18 * 2**20, transcendentals=512 * 512
        ),
        name="experts",
    )(
        blocks, tokens, router_weight, gate_weight[0], up_weight[0], down_weight[0]
    )
    tile = 512
    return pl.pallas_call(
        mix_kernel,
        grid=(tok_rows // tile,),
        out_shape=jax.ShapeDtypeStruct((tok_rows, feats), BF16),
        in_specs=[
            pl.BlockSpec((packed, 128), lambda i: (0, 0)),
            pl.BlockSpec((packed, feats), lambda i: (0, 0)),
        ],
        out_specs=pl.BlockSpec((tile, feats), lambda i: (i, 0)),
        scratch_shapes=[pltpu.VMEM((128, packed), F32)],
        compiler_params=pltpu.CompilerParams(vmem_limit_bytes=60 * 2**20),
        cost_estimate=pl.CostEstimate(
            flops=2 * tok_rows * packed * feats, bytes_accessed=6 * 2**20, transcendentals=0
        ),
        name="mix",
    )(index, back.reshape(packed, feats))


def shards(tokens, router_weight, gate_weight, up_weight, down_weight, picks):
    tok_rows = tokens.shape[0]
    flight, capacity = picks.shape
    blocks = picks.reshape(flight, DP, ROWS).transpose(1, 0, 2).reshape(DP, BLK)
    owners = blocks // tok_rows
    counts = jnp.sum(
        (owners[:, None, :] == jnp.arange(DP)[None, :, None]).astype(jnp.int32), axis=2
    )
    fits = jnp.max(counts) <= CAPS[0]
    args = (tokens, router_weight, gate_weight, up_weight, down_weight, blocks)
    return lax.cond(fits, lambda: kernel_shards(*args, CAPS[0]), lambda: kernel_shards(*args, CAPS[1]))


def solution(mesh):
    in_specs = (
        P("dp", "group"),
        P("group", None),
        P("group", None, "dp"),
        P("group", None, "dp"),
        P("group", "dp", None),
        P(),
    )
    out_specs = P("dp", "group")
    return jax.shard_map(shards, mesh=mesh, in_specs=in_specs, out_specs=out_specs, check_vma=False)
```

```python
import functools

import jax
import jax.numpy as jnp
from jax import lax
from jax.experimental import pallas as pl
from jax.experimental.pallas import tpu as pltpu
from jax.sharding import PartitionSpec as P

MESH = pl.DeviceIdType.MESH
BF16 = jnp.bfloat16
F32 = jnp.float32
DP = 16
GRP = 8
NEAR = 16
BLK = 256
ROWS = 32
HALF = 16


def iota(shape, dim, dtype=jnp.int32):
    out = lax.broadcasted_iota(jnp.int32, shape, dim)
    return out if dtype == jnp.int32 else out.astype(dtype)


def earlier(n):
    return ones(iota((n, n), 0) < iota((n, n), 1))


def ones(mask):
    return jnp.where(mask, 1.0, 0.0).astype(BF16)


def mm(a, b):
    return jnp.dot(a, b, preferred_element_type=F32)


def over(values):
    return jnp.sum(values, axis=0, keepdims=True)


def best(hit, value):
    return jnp.max(jnp.where(hit, value, -1.0), axis=1, keepdims=True)


def fill_onehot(onehot, index):
    rows = index.shape[0]
    high = jnp.floor(index * (1.0 / 128.0))
    lane = iota((rows, 128), 1, F32)
    low = ones(index - high * 128.0 == lane)
    high = high.astype(BF16)
    for t in range(onehot.shape[1] // 128):
        onehot[:, t * 128 : (t + 1) * 128] = jnp.where(high == float(t), low, 0.0).astype(BF16)


def place_picks(picks_ref, me, tok_rows, index_ref, spread, fit_ref):
    flight, cap = picks_ref.shape
    n_pair = flight * DP
    tri = earlier(cap)
    picks = picks_ref[...]
    owner = picks // tok_rows
    local = (picks - owner * tok_rows).astype(F32)
    dev = iota((DP, cap), 0)
    dev_f = dev.astype(F32)
    at_me = dev == me
    owned = [ones(dev == owner[q : q + 1]) for q in range(flight)]
    stacked = jnp.concatenate(owned, axis=0)
    owned = [o.astype(F32) for o in owned]
    before = mm(stacked, tri)
    count = mm(stacked, jnp.full((cap, cap), 1.0, BF16))
    room = jnp.maximum(ROWS - count, 0.0)
    r, c = iota((n_pair, n_pair), 0), iota((n_pair, n_pair), 1)
    turn = 2 * (r // DP) + 1
    in_turn = (c + DP - turn % DP) % DP < (r + DP - turn % DP) % DP
    room_before = mm(ones((r // DP == c // DP) & in_turn), room.astype(BF16))
    earlier_expert = ones((r % DP == c % DP) & (c // DP < r // DP))

    def of(values, q):
        return values[q * DP : (q + 1) * DP]

    rank = [over(owned[q] * of(before, q)) for q in range(flight)]
    extra = [rank[q] >= ROWS for q in range(flight)]
    extra_no = mm(jnp.concatenate([ones(e) for e in extra], axis=0), tri)
    mine = [owner[q : q + 1] == me for q in range(flight)]
    sends, takes, to_me, fits = [], [], [], jnp.zeros((DP, DP), F32)
    for q in range(flight):
        no = extra_no[q : q + 1]
        first = of(room_before, q)
        dest = jnp.where(
            extra[q] & (no >= first) & (no < first + of(room, q)), 1.0, 0.0
        )
        to_me.append(over(jnp.where(at_me, dest, 0.0)))
        sends.append(jnp.where(mine[q], dest, 0.0).astype(BF16))
        takes.append((owned[q] * to_me[q]).astype(BF16))
        fits = fits + lax.dot_general(
            owned[q].astype(BF16), dest.astype(BF16), (((1,), (1,)), ((), ())),
            preferred_element_type=F32,
        )
    fit_ref[...] = jnp.broadcast_to(jnp.max(fits, axis=(0, 1), keepdims=True), fit_ref.shape)

    def keys(hits):
        hits = jnp.concatenate(hits, axis=0)
        counts = mm(hits, jnp.full((cap, cap), 1.0, BF16)).astype(BF16)
        number = mm(hits, tri) + mm(earlier_expert, counts)
        hits = hits.astype(F32)
        return [over(of(hits, q) * (of(number, q) + NEAR * dev_f)) for q in range(flight)]

    n_far = DP * NEAR
    send_key, take_key = keys(sends), keys(takes)
    slot = iota((n_far, cap), 0, F32)
    far = jnp.full((n_far, cap), -1.0, F32)
    for q in range(flight):
        key = jnp.where(mine[q] & extra[q], send_key[q], -1.0)
        far = jnp.where(slot == key, local[q : q + 1], far)
    far = jnp.max(far, axis=1, keepdims=True)
    index_ref[pl.ds(BLK, n_far), :] = jnp.broadcast_to(far, (n_far, 128))
    slot = iota((ROWS, cap), 0, F32)
    column = iota((ROWS, n_far), 1, F32)
    for q in range(flight):
        key = jnp.where(mine[q], rank[q], -1.0)
        own = best(slot == key, local[q : q + 1])
        index_ref[pl.ds(q * ROWS, ROWS), :] = jnp.broadcast_to(own, (ROWS, 128))
        place = extra_no[q : q + 1] + over(
            jnp.where(at_me, of(count, q) - of(room_before, q), 0.0)
        )
        place = jnp.where(to_me[q] > 0.0, place, -1.0)
        source = best(slot == place, take_key[q])
        spread[pl.ds(q * ROWS, ROWS), :] = ones(source == column)


def expert_kernel(
    quick,
    picks_ref, tok_hbm, wr_hbm, wg_hbm, wu_hbm, wd_hbm,
    back_ref, index_ref, fit_ref,
    tok, wr, wg, wu, wd, onehot, packed, arrived, spread, rows, logit_part, logit_all,
    x, hidden, part, core_in, h0_in, h1_in, h1_edge, weighted, returned, outgoing,
    load_sem, own_sem,
    tok_ss, tok_rs, row_ss, row_rs, log_ss, log_rs, ag_ss, ag_rs, sib_ss, sib_rs,
    core_ss, core_rs, rs_ss, rs_rs, ret_ss, ret_rs, out_ss, out_rs,
):
    cap = packed.shape[1]
    d, g = lax.axis_index("dp"), lax.axis_index("group")
    y, xl, core = d // 4, (d // 2) % 2, d % 2
    tok_rows = tok.shape[0]
    feats = tok.shape[1]

    def block(yy, xx, cc):
        return (yy * 2 + xx) * 2 + cc

    up, down, far = (y + 1) % 4, (y + 3) % 4, (y + 2) % 4
    ox, oc = 1 - xl, 1 - core
    to_up = (block(up, xl, core), g)
    to_down = (block(down, xl, core), g)
    to_x = (block(y, ox, core), g)
    to_core = (block(y, xl, oc), g)

    sent = []

    def remote(src, dst, ss, rs, device):
        return pltpu.make_async_remote_copy(
            src_ref=src, dst_ref=dst, send_sem=ss, recv_sem=rs, device_id=device, device_id_type=MESH
        )

    def send(src, dst, ss, rs, device):
        copy = remote(src, dst, ss, rs, device)
        copy.start()
        sent.append(copy)
        return copy

    loads = []
    for i, (src, dst) in enumerate(
        ((tok_hbm, tok), (wr_hbm, wr), (wg_hbm, wg), (wu_hbm, wu), (wd_hbm, wd))
    ):
        copy = pltpu.make_async_copy(src, dst, load_sem.at[i])
        copy.start()
        loads.append(copy)

    barrier = pltpu.get_barrier_semaphore()
    for k in range(1, DP):
        pl.semaphore_signal(barrier, inc=1, device_id=((d + k) % DP, g), device_id_type=MESH)
    for k in range(1, GRP):
        pl.semaphore_signal(barrier, inc=1, device_id=(d, (g + k) % GRP), device_id_type=MESH)

    if quick:
        place_picks(picks_ref, d, tok_rows, index_ref, spread, fit_ref)
    else:
        tri = earlier(BLK)
        local = picks_ref[...] - d * tok_rows
        mine = (local >= 0) & (local < tok_rows)
        rank = jnp.dot(
            jnp.where(mine, 1.0, 0.0).astype(BF16), tri, preferred_element_type=F32
        )
        rank = jnp.where(mine, rank, -1.0)
        local = local.astype(F32)
        slot_rank = iota((cap, BLK), 0, F32)
        for b in range(DP):
            chosen = jnp.where(slot_rank == rank[b : b + 1, :], local[b : b + 1, :], -1.0)
            index = jnp.max(chosen, axis=1, keepdims=True)
            index_ref[pl.ds(b * cap, cap), :] = jnp.broadcast_to(index, (cap, 128))

        owner = picks_ref[pl.ds(d, 1), :] // tok_rows
        is_owner = jnp.where(iota((DP, BLK), 0) == owner, 1.0, 0.0)
        ranks = jnp.dot(is_owner.astype(BF16), tri, preferred_element_type=F32)
        place = jnp.sum(is_owner * ranks, axis=0, keepdims=True) + owner.astype(F32) * cap
        spread[...] = jnp.where(iota((DP * cap, BLK), 0, F32) == place, 1.0, 0.0).astype(BF16)
        fit_ref[...] = jnp.zeros_like(fit_ref)

    loads[0].wait()
    pl.semaphore_wait(barrier, DP - 1 + GRP - 1)
    if quick:
        fill_onehot(onehot, index_ref[pl.ds(BLK, DP * cap), :])
        packed[...] = mm(onehot[...], tok[...]).astype(BF16).reshape(DP, cap, feats)
        for k in range(1, DP):
            to = (d + k) % DP
            send(packed.at[to], arrived.at[d], tok_ss.at[k], tok_rs.at[k], (to, g))
        arrived[d] = jnp.zeros((cap, feats), BF16)
        fill_onehot(onehot, index_ref[pl.ds(0, BLK), :])
        kept = mm(onehot[...], tok[...])
    else:

        def gather(step, carry):
            first = (d + 1 + step) % DP
            fill_onehot(onehot, index_ref[pl.ds(pl.multiple_of(first * cap, 16), cap), :])
            packed[first] = mm(onehot[...], tok[...]).astype(BF16)
            k = (first - d + DP) % DP

            @pl.when(first != d)
            def _():
                remote(packed.at[first], arrived.at[d], tok_ss.at[k], tok_rs.at[k], (first, g)).start()

            return carry

        lax.fori_loop(0, DP, gather, 0)
        own = pltpu.make_async_copy(packed.at[d], arrived.at[d], own_sem.at[0])
        own.start()
        own.wait()
    loads[1].wait()
    hi = wr[...].astype(BF16)
    lo = (wr[...] - hi.astype(F32)).astype(BF16)
    for k in range(1, DP):
        frm = (d - k + DP) % DP
        remote(packed.at[frm], arrived.at[frm], tok_ss.at[k], tok_rs.at[k], (frm, g)).wait_recv()

    came = arrived[...].reshape(DP * cap, feats)
    if quick:
        taken = (mm(spread[...], came) + kept).astype(BF16)
    else:
        taken = lax.dot_general(
            spread[...], came, (((0,), (0,)), ((), ())), preferred_element_type=F32
        ).astype(BF16)
    rows[...] = taken.reshape(GRP, ROWS, feats)
    mine_cols = pl.ds(pl.multiple_of(g * feats, feats), feats)
    for k in range(1, GRP):
        q = (g + k) % GRP
        send(rows.at[q], x.at[d, :, mine_cols], row_ss.at[k], row_rs.at[k], (d, q))
    own = pltpu.make_async_copy(rows.at[g], x.at[d, :, mine_cols], own_sem.at[1])
    own.start()
    logits = jnp.dot(taken, hi, preferred_element_type=F32) + jnp.dot(
        taken, lo, preferred_element_type=F32
    )
    logit_part[...] = logits.reshape(GRP, ROWS, logits.shape[1])
    own.wait()
    for k in range(1, GRP):
        frm = (g - k + GRP) % GRP
        cols = pl.ds(pl.multiple_of(frm * feats, feats), feats)
        remote(rows.at[frm], x.at[d, :, cols], row_ss.at[k], row_rs.at[k], (d, frm)).wait_recv()

    h0, h1 = pl.ds(0, HALF), pl.ds(HALF, HALF)
    wide = x.shape[2]
    left, right = pl.ds(0, wide // 2), pl.ds(wide // 2, wide // 2)

    def ag(i, b, half, to, cols=None):
        ref = x.at[b, half] if cols is None else x.at[b, half, cols]
        return send(ref, ref, ag_ss.at[i], ag_rs.at[i], to)

    def got(i, b, half, cols=None):
        ref = x.at[b, half] if cols is None else x.at[b, half, cols]
        remote(ref, ref, ag_ss.at[i], ag_rs.at[i], to_x).wait_recv()

    n_sib = [0]

    def sib(b, half):
        ref = x.at[b, half]
        send(ref, ref, sib_ss.at[n_sib[0]], sib_rs.at[n_sib[0]], to_core)
        n_sib[0] += 1

    own_b, x_b = block(y, xl, core), block(y, ox, core)
    up_b, down_b, far_b = block(up, xl, core), block(down, xl, core), block(far, xl, core)
    up_x, down_x, far_x = block(up, ox, core), block(down, ox, core), block(far, ox, core)
    ag(0, own_b, h0, to_x)
    ag(7, own_b, h1, to_up)
    ag(8, own_b, h1, to_down)
    ag(1, own_b, h0, to_up)
    ag(2, own_b, h0, to_down)
    ag(9, own_b, h1, to_x)
    sib(own_b, h0)
    sib(own_b, h1)
    for k in range(1, GRP):
        q = (g + k) % GRP
        send(logit_part.at[q], logit_all.at[g], log_ss.at[k], log_rs.at[k], (d, q))
    own2 = pltpu.make_async_copy(logit_part.at[g], logit_all.at[g], own_sem.at[2])
    own2.start()
    got(0, x_b, h0)
    ag(3, x_b, h0, to_up)
    ag(4, x_b, h0, to_down)
    sib(x_b, h0)
    got(7, down_b, h1)
    ag(10, down_b, h1, to_up, left)
    ag(12, down_b, h1, to_x)
    sib(down_b, h1)
    got(8, up_b, h1)
    ag(11, up_b, h1, to_down, right)
    ag(13, up_b, h1, to_x)
    sib(up_b, h1)
    got(1, down_b, h0)
    ag(5, down_b, h0, to_up)
    sib(down_b, h0)
    got(2, up_b, h0)
    sib(up_b, h0)
    got(9, x_b, h1)
    sib(x_b, h1)
    got(4, up_x, h0)
    ag(6, up_x, h0, to_down)
    sib(up_x, h0)
    got(3, down_x, h0)
    sib(down_x, h0)
    got(10, far_b, h1, left)
    got(11, far_b, h1, right)
    ag(14, far_b, h1, to_x)
    sib(far_b, h1)
    got(12, down_x, h1)
    sib(down_x, h1)
    got(13, up_x, h1)
    sib(up_x, h1)
    got(5, far_b, h0)
    sib(far_b, h0)
    got(6, far_x, h0)
    sib(far_x, h0)
    got(14, far_x, h1)
    sib(far_x, h1)
    n_sib[0] = 0
    for i in range(16):
        ref = x.at[block(y, xl, oc), h0]
        remote(ref, ref, sib_ss.at[i], sib_rs.at[i], to_core).wait_recv()

    loads[2].wait()
    loads[3].wait()
    n_rows = DP * ROWS
    units = wg.shape[1]

    def into_hidden(step, carry):
        m = step // 2
        cols = pl.ds(pl.multiple_of((step % 2) * (units // 2), 128), units // 2)
        xs = x[pl.ds(m * 8, 8)].reshape(n_rows // 2, wide)
        gate = jnp.dot(xs, wg[:, cols], preferred_element_type=F32)
        lift = jnp.dot(xs, wu[:, cols], preferred_element_type=F32)
        value = gate / (1.0 + jnp.exp(-gate)) * lift
        hidden[pl.ds(pl.multiple_of(m * (n_rows // 2), 16), n_rows // 2), cols] = value.astype(BF16)
        return carry

    lax.fori_loop(0, 4, into_hidden, 0)
    loads[4].wait()

    def out_of_hidden(yy):
        hs = hidden[pl.ds(pl.multiple_of(yy * 4 * ROWS, 16), 4 * ROWS), :]

        def tile(step, carry):
            cols = pl.ds(pl.multiple_of(step * 512, 512), 512)
            value = jnp.dot(hs, wd[:, cols], preferred_element_type=F32).astype(BF16)
            part[pl.ds(yy * 4, 4), :, cols] = value.reshape(4, ROWS, 512)
            return carry

        lax.fori_loop(0, wide // 512, tile, 0)

    def to_sibling(i, yy):
        for xx in range(2):
            send(
                part.at[block(yy, xx, oc)], core_in.at[yy * 2 + xx],
                core_ss.at[2 * i + xx], core_rs.at[2 * i + xx], to_core,
            )

    def add_sibling(i, yy):
        for xx in range(2):
            b = block(yy, xx, core)
            remote(
                part.at[b], core_in.at[yy * 2 + xx],
                core_ss.at[2 * i + xx], core_rs.at[2 * i + xx], to_core,
            ).wait_recv()
            part[b] = (part[b].astype(F32) + core_in[yy * 2 + xx].astype(F32)).astype(BF16)

    def rs(i, src, dst, to):
        send(src, dst, rs_ss.at[i], rs_rs.at[i], to)

    def rs_got(i, dst):
        remote(dst, dst, rs_ss.at[i], rs_rs.at[i], to_x).wait_recv()

    def add(b, half, ref, cols=None):
        if cols is None:
            part[b, half] = (part[b, half].astype(F32) + ref[...].astype(F32)).astype(BF16)
        else:
            part[b, half, cols] = (part[b, half, cols].astype(F32) + ref[...].astype(F32)).astype(BF16)

    out_of_hidden(far)
    to_sibling(0, far)
    out_of_hidden(up)
    to_sibling(1, up)
    add_sibling(0, far)
    rs(0, part.at[far_b, h0], h0_in.at[0], to_up)
    rs(1, part.at[far_x, h0], h0_in.at[1], to_down)
    rs(7, part.at[far_x, h1], h1_in.at[0], to_x)
    out_of_hidden(down)
    to_sibling(2, down)
    add_sibling(1, up)
    rs(2, part.at[up_x, h0], h0_in.at[2], to_up)
    rs(8, part.at[up_x, h1], h1_in.at[1], to_x)
    rs_got(7, h1_in.at[0])
    add(far_b, h1, h1_in.at[0])
    rs(9, part.at[far_b, h1, left], h1_edge.at[0], to_up)
    rs(10, part.at[far_b, h1, right], h1_edge.at[1], to_down)
    out_of_hidden(y)
    to_sibling(3, y)
    add_sibling(2, down)
    rs(3, part.at[down_b, h0], h0_in.at[3], to_down)
    rs(11, part.at[down_x, h1], h1_in.at[2], to_x)
    rs_got(0, h0_in.at[0])
    add(up_b, h0, h0_in.at[0])
    rs(4, part.at[up_b, h0], h0_in.at[4], to_up)
    rs_got(1, h0_in.at[1])
    add(down_x, h0, h0_in.at[1])
    rs(5, part.at[down_x, h0], h0_in.at[5], to_down)
    rs_got(8, h1_in.at[1])
    add(up_b, h1, h1_in.at[1])
    rs_got(9, h1_edge.at[0])
    add(up_b, h1, h1_edge.at[0], left)
    rs(12, part.at[up_b, h1], h1_in.at[4], to_up)
    rs_got(11, h1_in.at[2])
    add(down_b, h1, h1_in.at[2])
    rs_got(10, h1_edge.at[1])
    add(down_b, h1, h1_edge.at[1], right)
    rs(13, part.at[down_b, h1], h1_in.at[5], to_down)
    add_sibling(3, y)
    rs(14, part.at[x_b, h1], h1_in.at[3], to_x)

    own2.wait()
    for k in range(1, GRP):
        frm = (g - k + GRP) % GRP
        remote(logit_part.at[frm], logit_all.at[frm], log_ss.at[k], log_rs.at[k], (d, frm)).wait_recv()
    logits = logit_all[0]
    for q in range(1, GRP):
        logits = logits + logit_all[q]
    n_exp = logits.shape[1]
    grown = jnp.exp(logits - jnp.max(logits, axis=1, keepdims=True))
    column = iota(logits.shape, 1) == g * (n_exp // GRP)
    prob = jnp.sum(jnp.where(column, grown, 0.0), axis=1, keepdims=True) / jnp.sum(
        grown, axis=1, keepdims=True
    )

    rs_got(2, h0_in.at[2])
    rs_got(5, h0_in.at[5])
    part[x_b, h0] = (
        part[x_b, h0].astype(F32) + h0_in[2].astype(F32) + h0_in[5].astype(F32)
    ).astype(BF16)
    rs(6, part.at[x_b, h0], h0_in.at[6], to_x)
    rs_got(3, h0_in.at[3])
    rs_got(4, h0_in.at[4])
    first = part[own_b, h0].astype(F32) + h0_in[3].astype(F32) + h0_in[4].astype(F32)
    rs_got(6, h0_in.at[6])
    first = (first + h0_in[6].astype(F32)).astype(BF16).astype(F32)
    weighted[h0] = (first * prob[:HALF]).astype(BF16)
    rs_got(14, h1_in.at[3])
    rs_got(12, h1_in.at[4])
    rs_got(13, h1_in.at[5])
    second = part[own_b, h1].astype(F32) + h1_in[3].astype(F32)
    second = second + h1_in[4].astype(F32) + h1_in[5].astype(F32)
    weighted[h1] = (second.astype(BF16).astype(F32) * prob[HALF:]).astype(BF16)

    mine_rows = pl.ds(pl.multiple_of(g * ROWS, ROWS), ROWS)
    for k in range(1, GRP):
        q = (g + k) % GRP
        cols = pl.ds(pl.multiple_of(q * feats, feats), feats)
        send(weighted.at[:, cols], returned.at[mine_rows], ret_ss.at[k], ret_rs.at[k], (d, q))
    own = pltpu.make_async_copy(weighted.at[:, mine_cols], returned.at[mine_rows], own_sem.at[3])
    own.start()
    own.wait()
    for k in range(1, GRP):
        frm = (g - k + GRP) % GRP
        frm_rows = returned.at[pl.ds(pl.multiple_of(frm * ROWS, ROWS), ROWS)]
        remote(frm_rows, frm_rows, ret_ss.at[k], ret_rs.at[k], (d, frm)).wait_recv()

    block_rows = returned[...]
    if quick:
        base = BLK
        kept_home = pltpu.make_async_copy(returned, back_ref.at[pl.ds(0, BLK)], own_sem.at[1])
        kept_home.start()
        back = lax.dot_general(
            spread[...], block_rows, (((0,), (0,)), ((), ())), preferred_element_type=F32
        )
    else:
        base = 0
        back = mm(spread[...], block_rows)
    outgoing[...] = back.astype(BF16).reshape(DP, cap, feats)
    to_rows = back_ref.at[pl.ds(pl.multiple_of(base + d * cap, 16), cap)]
    for k in range(1, DP):
        to = (d + k) % DP
        send(outgoing.at[to], to_rows, out_ss.at[k], out_rs.at[k], (to, g))
    own = pltpu.make_async_copy(outgoing.at[d], to_rows, own_sem.at[4])
    own.start()
    own.wait()
    if quick:
        kept_home.wait()
    for k in range(1, DP):
        frm = (d - k + DP) % DP
        frm_rows = back_ref.at[pl.ds(pl.multiple_of(base + frm * cap, 16), cap)]
        remote(outgoing.at[frm], frm_rows, out_ss.at[k], out_rs.at[k], (frm, g)).wait_recv()

    if not quick:
        for k in range(1, DP):
            to = (d + k) % DP
            remote(packed.at[to], arrived.at[d], tok_ss.at[k], tok_rs.at[k], (to, g)).wait_send()
    for copy in sent:
        copy.wait_send()


def mix_kernel(index_ref, back_ref, out_ref, high, low):
    tile = out_ref.shape[0]

    @pl.when(pl.program_id(0) == 0)
    def _():
        index = index_ref[...].T
        top = jnp.floor(index * (1.0 / 128.0))
        high[...] = top.astype(BF16)
        low[...] = ones(index - top * 128.0 == iota(index.shape, 0, F32))

    first = (pl.program_id(0) * (tile // 128)).astype(F32)
    like = (1, high.shape[1])
    parts = [
        jnp.where(high[...] == jnp.full(like, first + float(t), F32).astype(BF16), low[...], 0.0)
        for t in range(tile // 128)
    ]
    out_ref[...] = mm(jnp.concatenate(parts, axis=0), back_ref[...]).astype(BF16)


def route(tokens, router_weight, gate_weight, up_weight, down_weight, picks, quick):
    cap = NEAR if quick else BLK
    packed = DP * cap
    n_back = packed + (BLK if quick else 0)
    tok_rows, feats = tokens.shape
    units, wide = down_weight.shape[1:]
    n_exp = router_weight.shape[1]
    dma = pltpu.SemaphoreType.DMA
    any_spec = pl.BlockSpec(memory_space=pl.ANY)
    vmem_spec = pl.BlockSpec(memory_space=pltpu.VMEM)
    return pl.pallas_call(
        functools.partial(expert_kernel, quick),
        out_shape=(
            jax.ShapeDtypeStruct((n_back, feats), BF16),
            jax.ShapeDtypeStruct((n_back, 128), F32),
            jax.ShapeDtypeStruct((8, 128), F32),
        ),
        in_specs=[vmem_spec] + [any_spec] * 5,
        out_specs=(any_spec, vmem_spec, vmem_spec),
        scratch_shapes=[
            pltpu.VMEM((tok_rows, feats), BF16),
            pltpu.VMEM((feats, n_exp), F32),
            pltpu.VMEM((wide, units), BF16),
            pltpu.VMEM((wide, units), BF16),
            pltpu.VMEM((units, wide), BF16),
            pltpu.VMEM((BLK, tok_rows), BF16),
            pltpu.VMEM((DP, cap, feats), BF16),
            pltpu.VMEM((DP, cap, feats), BF16),
            pltpu.VMEM((BLK, packed) if quick else (packed, BLK), BF16),
            pltpu.VMEM((GRP, ROWS, feats), BF16),
            pltpu.VMEM((GRP, ROWS, n_exp), F32),
            pltpu.VMEM((GRP, ROWS, n_exp), F32),
            pltpu.VMEM((DP, ROWS, wide), BF16),
            pltpu.VMEM((DP * ROWS, units), BF16),
            pltpu.VMEM((DP, ROWS, wide), BF16),
            pltpu.VMEM((DP // 2, ROWS, wide), BF16),
            pltpu.VMEM((7, HALF, wide), BF16),
            pltpu.VMEM((6, HALF, wide), BF16),
            pltpu.VMEM((2, HALF, wide // 2), BF16),
            pltpu.VMEM((ROWS, wide), BF16),
            pltpu.VMEM((BLK, feats), BF16),
            pltpu.VMEM((DP, cap, feats), BF16),
            dma((5,)),
            dma((5,)),
            dma((DP,)), dma((DP,)),
            dma((GRP,)), dma((GRP,)),
            dma((GRP,)), dma((GRP,)),
            dma((15,)), dma((15,)),
            dma((16,)), dma((16,)),
            dma((8,)), dma((8,)),
            dma((15,)), dma((15,)),
            dma((GRP,)), dma((GRP,)),
            dma((DP,)), dma((DP,)),
        ],
        compiler_params=pltpu.CompilerParams(
            collective_id=1 if quick else 2, has_side_effects=True, vmem_limit_bytes=60 * 2**20
        ),
        cost_estimate=pl.CostEstimate(
            flops=11 * 10**9, bytes_accessed=18 * 2**20, transcendentals=512 * 512
        ),
        name="experts" if quick else "experts_any",
    )(
        picks, tokens, router_weight, gate_weight[0], up_weight[0], down_weight[0]
    )


def mix(back, index, tok_rows):
    rows, feats = back.shape
    tile = 512
    return pl.pallas_call(
        mix_kernel,
        grid=(tok_rows // tile,),
        out_shape=jax.ShapeDtypeStruct((tok_rows, feats), BF16),
        in_specs=[
            pl.BlockSpec((rows, 128), lambda i: (0, 0)),
            pl.BlockSpec((rows, feats), lambda i: (0, 0)),
        ],
        out_specs=pl.BlockSpec((tile, feats), lambda i: (i, 0)),
        scratch_shapes=[pltpu.VMEM((128, rows), BF16), pltpu.VMEM((128, rows), BF16)],
        compiler_params=pltpu.CompilerParams(vmem_limit_bytes=60 * 2**20),
        cost_estimate=pl.CostEstimate(
            flops=2 * tok_rows * rows * feats, bytes_accessed=6 * 2**20, transcendentals=0
        ),
        name="mix",
    )(index, back)


def shards(tokens, router_weight, gate_weight, up_weight, down_weight, picks):
    tok_rows = tokens.shape[0]
    flight, capacity = picks.shape
    args = (tokens, router_weight, gate_weight, up_weight, down_weight)
    back, index, fit = route(*args, picks, True)

    def any_picks():
        blocks = picks.reshape(flight, DP, ROWS).transpose(1, 0, 2).reshape(DP, BLK)
        back, index, _ = route(*args, blocks, False)
        return mix(back, index, tok_rows)

    return lax.cond(fit[0, 0] <= NEAR, lambda: mix(back, index, tok_rows), any_picks)


def solution(mesh):
    in_specs = (
        P("dp", "group"),
        P("group", None),
        P("group", None, "dp"),
        P("group", None, "dp"),
        P("group", "dp", None),
        P(),
    )
    out_specs = P("dp", "group")
    return jax.shard_map(shards, mesh=mesh, in_specs=in_specs, out_specs=out_specs, check_vma=False)
```

```python
import functools

import jax
import jax.numpy as jnp
from jax import lax
from jax.experimental import pallas as pl
from jax.experimental.pallas import tpu as pltpu
from jax.sharding import PartitionSpec as P

MESH = pl.DeviceIdType.MESH
BF16 = jnp.bfloat16
F32 = jnp.float32
DP = 16
GRP = 8
NEAR = 16
BLK = 256
ROWS = 32
HALF = 16


def iota(shape, dim, dtype=jnp.int32):
    out = lax.broadcasted_iota(jnp.int32, shape, dim)
    return out if dtype == jnp.int32 else out.astype(dtype)


def earlier(n):
    return ones(iota((n, n), 0) < iota((n, n), 1))


def ones(mask):
    return jnp.where(mask, 1.0, 0.0).astype(BF16)


def mm(a, b):
    return jnp.dot(a, b, preferred_element_type=F32)


def over(values):
    return jnp.sum(values, axis=0, keepdims=True)


def best(hit, value):
    return jnp.max(jnp.where(hit, value, -1.0), axis=1, keepdims=True)


def fill_onehot(onehot, index):
    rows = index.shape[0]
    high = jnp.floor(index * (1.0 / 128.0))
    lane = iota((rows, 128), 1, F32)
    low = ones(index - high * 128.0 == lane)
    high = high.astype(BF16)
    for t in range(onehot.shape[1] // 128):
        onehot[:, t * 128 : (t + 1) * 128] = jnp.where(high == float(t), low, 0.0).astype(BF16)


def place_picks(picks_ref, me, tok_rows, index_ref, spread, fit_ref):
    flight, cap = picks_ref.shape
    n_pair = flight * DP
    tri = earlier(cap)
    picks = picks_ref[...]
    owner = picks // tok_rows
    local = (picks - owner * tok_rows).astype(F32)
    dev = iota((DP, cap), 0)
    dev_f = dev.astype(F32)
    at_me = dev == me
    owned = [ones(dev == owner[q : q + 1]) for q in range(flight)]
    stacked = jnp.concatenate(owned, axis=0)
    owned = [o.astype(F32) for o in owned]
    before = mm(stacked, tri)
    count = mm(stacked, jnp.full((cap, cap), 1.0, BF16))
    room = jnp.maximum(ROWS - count, 0.0)
    r, c = iota((n_pair, n_pair), 0), iota((n_pair, n_pair), 1)
    turn = 2 * (r // DP) + 1
    in_turn = (c + DP - turn % DP) % DP < (r + DP - turn % DP) % DP
    room_before = mm(ones((r // DP == c // DP) & in_turn), room.astype(BF16))
    earlier_expert = ones((r % DP == c % DP) & (c // DP < r // DP))

    def of(values, q):
        return values[q * DP : (q + 1) * DP]

    rank = [over(owned[q] * of(before, q)) for q in range(flight)]
    extra = [rank[q] >= ROWS for q in range(flight)]
    extra_no = mm(jnp.concatenate([ones(e) for e in extra], axis=0), tri)
    mine = [owner[q : q + 1] == me for q in range(flight)]
    sends, takes, to_me, fits = [], [], [], jnp.zeros((DP, DP), F32)
    for q in range(flight):
        no = extra_no[q : q + 1]
        first = of(room_before, q)
        dest = jnp.where(
            extra[q] & (no >= first) & (no < first + of(room, q)), 1.0, 0.0
        )
        to_me.append(over(jnp.where(at_me, dest, 0.0)))
        sends.append(jnp.where(mine[q], dest, 0.0).astype(BF16))
        takes.append((owned[q] * to_me[q]).astype(BF16))
        fits = fits + lax.dot_general(
            owned[q].astype(BF16), dest.astype(BF16), (((1,), (1,)), ((), ())),
            preferred_element_type=F32,
        )
    fit_ref[0, 0] = jnp.max(fits)

    def keys(hits):
        hits = jnp.concatenate(hits, axis=0)
        counts = mm(hits, jnp.full((cap, cap), 1.0, BF16)).astype(BF16)
        number = mm(hits, tri) + mm(earlier_expert, counts)
        hits = hits.astype(F32)
        return [over(of(hits, q) * (of(number, q) + NEAR * dev_f)) for q in range(flight)]

    n_far = DP * NEAR
    send_key, take_key = keys(sends), keys(takes)
    slot = iota((n_far, cap), 0, F32)
    far = jnp.full((n_far, cap), -1.0, F32)
    for q in range(flight):
        key = jnp.where(mine[q] & extra[q], send_key[q], -1.0)
        far = jnp.where(slot == key, local[q : q + 1], far)
    far = jnp.max(far, axis=1, keepdims=True)
    index_ref[pl.ds(BLK, n_far), :] = jnp.broadcast_to(far, (n_far, 128))
    slot = iota((ROWS, cap), 0, F32)
    column = iota((ROWS, n_far), 1, F32)
    for q in range(flight):
        key = jnp.where(mine[q], rank[q], -1.0)
        own = best(slot == key, local[q : q + 1])
        index_ref[pl.ds(q * ROWS, ROWS), :] = jnp.broadcast_to(own, (ROWS, 128))
        place = extra_no[q : q + 1] + over(
            jnp.where(at_me, of(count, q) - of(room_before, q), 0.0)
        )
        place = jnp.where(to_me[q] > 0.0, place, -1.0)
        source = best(slot == place, take_key[q])
        spread[pl.ds(q * ROWS, ROWS), :] = ones(source == column)


def expert_kernel(
    quick,
    picks_ref, tok_hbm, wr_hbm, wg_hbm, wu_hbm, wd_hbm,
    back_ref, high_ref, low_ref, fit_ref,
    index_ref, tok, wr, wg, wu, wd, onehot, packed, arrived, spread, rows, logit_part, logit_all,
    x, hidden, part, core_in, sum_in, weighted, returned, outgoing,
    load_sem, own_sem,
    tok_ss, tok_rs, row_ss, row_rs, log_ss, log_rs, ag_ss, ag_rs, sib_ss, sib_rs,
    core_ss, core_rs, rs_ss, rs_rs, ret_ss, ret_rs, out_ss, out_rs,
):
    cap = packed.shape[1]
    d, g = lax.axis_index("dp"), lax.axis_index("group")
    y, xl, core = d // 4, (d // 2) % 2, d % 2
    tok_rows = tok.shape[0]
    feats = tok.shape[1]

    def block(yy, xx, cc):
        return (yy * 2 + xx) * 2 + cc

    up, down, far = (y + 1) % 4, (y + 3) % 4, (y + 2) % 4
    ox, oc = 1 - xl, 1 - core
    to_up = (block(up, xl, core), g)
    to_down = (block(down, xl, core), g)
    to_x = (block(y, ox, core), g)
    to_core = (block(y, xl, oc), g)

    sent = []

    def remote(src, dst, ss, rs, device):
        return pltpu.make_async_remote_copy(
            src_ref=src, dst_ref=dst, send_sem=ss, recv_sem=rs, device_id=device, device_id_type=MESH
        )

    def send(src, dst, ss, rs, device):
        copy = remote(src, dst, ss, rs, device)
        copy.start()
        sent.append(copy)
        return copy

    loads = []
    for i, (src, dst) in enumerate(
        ((tok_hbm, tok), (wr_hbm, wr), (wg_hbm, wg), (wu_hbm, wu), (wd_hbm, wd))
    ):
        copy = pltpu.make_async_copy(src, dst, load_sem.at[i])
        if i < 1:
            copy.start()
        loads.append(copy)

    barrier = pltpu.get_barrier_semaphore()
    for k in range(1, DP):
        pl.semaphore_signal(barrier, inc=1, device_id=((d + k) % DP, g), device_id_type=MESH)
    for k in range(1, GRP):
        pl.semaphore_signal(barrier, inc=1, device_id=(d, (g + k) % GRP), device_id_type=MESH)

    if quick:
        place_picks(picks_ref, d, tok_rows, index_ref, spread, fit_ref)
    else:
        tri = earlier(BLK)
        local = picks_ref[...] - d * tok_rows
        mine = (local >= 0) & (local < tok_rows)
        rank = jnp.dot(
            jnp.where(mine, 1.0, 0.0).astype(BF16), tri, preferred_element_type=F32
        )
        rank = jnp.where(mine, rank, -1.0)
        local = local.astype(F32)
        slot_rank = iota((cap, BLK), 0, F32)
        for b in range(DP):
            chosen = jnp.where(slot_rank == rank[b : b + 1, :], local[b : b + 1, :], -1.0)
            index = jnp.max(chosen, axis=1, keepdims=True)
            index_ref[pl.ds(b * cap, cap), :] = jnp.broadcast_to(index, (cap, 128))

        owner = picks_ref[pl.ds(d, 1), :] // tok_rows
        is_owner = jnp.where(iota((DP, BLK), 0) == owner, 1.0, 0.0)
        ranks = jnp.dot(is_owner.astype(BF16), tri, preferred_element_type=F32)
        place = jnp.sum(is_owner * ranks, axis=0, keepdims=True) + owner.astype(F32) * cap
        spread[...] = jnp.where(iota((DP * cap, BLK), 0, F32) == place, 1.0, 0.0).astype(BF16)
        fit_ref[0, 0] = 0.0

    loads[0].wait()
    for copy in loads[1:]:
        copy.start()
    if quick:
        fill_onehot(onehot, index_ref[pl.ds(BLK, DP * cap), :])
        packed[...] = mm(onehot[...], tok[...]).astype(BF16).reshape(DP, cap, feats)
        pl.semaphore_wait(barrier, DP - 1 + GRP - 1)
        for k in range(1, DP):
            to = (d + k) % DP
            send(packed.at[to], arrived.at[d], tok_ss.at[k], tok_rs.at[k], (to, g))
        arrived[d] = jnp.zeros((cap, feats), BF16)
        fill_onehot(onehot, index_ref[pl.ds(0, BLK), :])
        kept = mm(onehot[...], tok[...])
    else:
        pl.semaphore_wait(barrier, DP - 1 + GRP - 1)

        def gather(step, carry):
            first = (d + 1 + step) % DP
            fill_onehot(onehot, index_ref[pl.ds(pl.multiple_of(first * cap, 16), cap), :])
            packed[first] = mm(onehot[...], tok[...]).astype(BF16)
            k = (first - d + DP) % DP

            @pl.when(first != d)
            def _():
                remote(packed.at[first], arrived.at[d], tok_ss.at[k], tok_rs.at[k], (first, g)).start()

            return carry

        lax.fori_loop(0, DP, gather, 0)
        own = pltpu.make_async_copy(packed.at[d], arrived.at[d], own_sem.at[6])
        own.start()
        own.wait()
    loads[1].wait()
    hi = wr[...].astype(BF16)
    lo = (wr[...] - hi.astype(F32)).astype(BF16)
    for k in range(1, DP):
        frm = (d - k + DP) % DP
        remote(packed.at[frm], arrived.at[frm], tok_ss.at[k], tok_rs.at[k], (frm, g)).wait_recv()

    came = arrived[...].reshape(DP * cap, feats)
    if quick:
        taken = (mm(spread[...], came) + kept).astype(BF16)
    else:
        taken = lax.dot_general(
            spread[...], came, (((0,), (0,)), ((), ())), preferred_element_type=F32
        ).astype(BF16)
    rows[...] = taken.reshape(GRP, ROWS, feats)
    mine_cols = pl.ds(pl.multiple_of(g * feats, feats), feats)
    yx = y * 2 + xl

    def half_rows(f):
        return pl.ds(f * HALF, HALF)

    for f in range(2):
        for k in range(1, GRP):
            q = (g + k) % GRP
            send(
                rows.at[q, half_rows(f)], x.at[f, yx, core, :, mine_cols],
                row_ss.at[f, k], row_rs.at[f, k], (d, q),
            )
    own_rows = []
    for f in range(2):
        copy = pltpu.make_async_copy(
            rows.at[g, half_rows(f)], x.at[f, yx, core, :, mine_cols], own_sem.at[f]
        )
        copy.start()
        own_rows.append(copy)
    logits = mm(taken, hi) + mm(taken, lo)
    logit_part[...] = logits.reshape(GRP, ROWS, logits.shape[1])

    wide = x.shape[4]
    units = wg.shape[1]
    n_half = DP * HALF
    quarter = wide // 4
    left, right = pl.ds(0, 2 * quarter), pl.ds(2 * quarter, 2 * quarter)
    right_a, right_b = pl.ds(2 * quarter, quarter), pl.ds(3 * quarter, quarter)
    own_p, x_p = y * 2 + xl, y * 2 + ox
    up_p, down_p, far_p = up * 2 + xl, down * 2 + xl, far * 2 + xl
    up_x, down_x, far_x = up * 2 + ox, down * 2 + ox, far * 2 + ox
    at_place = (own_p, x_p, up_p, up_x, down_p, down_x, far_p, far_x)

    def ag(f, i, p, cols, to):
        ref = x.at[f, p, core, :, cols]
        send(ref, ref, ag_ss.at[f, i], ag_rs.at[f, i], to)

    def got(f, i, p, cols):
        ref = x.at[f, p, core, :, cols]
        remote(ref, ref, ag_ss.at[f, i], ag_rs.at[f, i], to_x).wait_recv()

    def sib(f, p, cols):
        i = [n for n in range(8) if at_place[n] is p][0] * 2 + (cols is right)
        ref = x.at[f, p, core, :, cols]
        send(ref, ref, sib_ss.at[f, i], sib_rs.at[f, i], to_core)

    def sibs(f):
        for i in range(16):
            ref = x.at[f, at_place[i // 2], oc, :, (left, right)[i % 2]]
            remote(ref, ref, sib_ss.at[f, i], sib_rs.at[f, i], to_core).wait_recv()

    def own_out(f):
        own_rows[f].wait()
        for k in range(1, GRP):
            frm = (g - k + GRP) % GRP
            cols = pl.ds(pl.multiple_of(frm * feats, feats), feats)
            remote(
                rows.at[frm, half_rows(f)], x.at[f, yx, core, :, cols],
                row_ss.at[f, k], row_rs.at[f, k], (d, frm),
            ).wait_recv()
        ag(f, 0, own_p, left, to_x)
        ag(f, 7, own_p, right, to_up)
        ag(f, 8, own_p, right, to_down)
        ag(f, 1, own_p, left, to_up)
        ag(f, 2, own_p, left, to_down)
        ag(f, 9, own_p, right, to_x)
        sib(f, own_p, left)
        sib(f, own_p, right)

    def relay_near(f):
        got(f, 0, x_p, left)
        ag(f, 3, x_p, left, to_up)
        ag(f, 4, x_p, left, to_down)
        sib(f, x_p, left)
        got(f, 8, up_p, right)
        ag(f, 11, up_p, right_b, to_down)
        ag(f, 13, up_p, right, to_x)
        sib(f, up_p, right)
        got(f, 7, down_p, right)
        ag(f, 10, down_p, right_a, to_up)
        ag(f, 12, down_p, right, to_x)
        sib(f, down_p, right)

    def relay_left(f):
        got(f, 1, down_p, left)
        ag(f, 5, down_p, left, to_up)
        sib(f, down_p, left)
        got(f, 2, up_p, left)
        sib(f, up_p, left)
        got(f, 9, x_p, right)
        sib(f, x_p, right)

    def relay_far(f):
        got(f, 4, up_x, left)
        ag(f, 6, up_x, left, to_down)
        sib(f, up_x, left)
        got(f, 10, far_p, right_a)
        got(f, 11, far_p, right_b)
        ag(f, 14, far_p, right, to_x)
        sib(f, far_p, right)

    def last_near(f):
        got(f, 3, down_x, left)
        sib(f, down_x, left)
        got(f, 13, up_x, right)
        sib(f, up_x, right)
        got(f, 12, down_x, right)
        sib(f, down_x, right)

    def last_far(f):
        got(f, 5, far_p, left)
        sib(f, far_p, left)
        got(f, 6, far_x, left)
        sib(f, far_x, left)
        got(f, 14, far_x, right)
        sib(f, far_x, right)

    def into_hidden(f, step):
        cols = pl.ds(step * (units // 2), units // 2)
        xs = x[f].reshape(n_half, wide)
        gate = mm(xs, wg[:, cols])
        lift = mm(xs, wu[:, cols])
        hidden[f, :, cols] = (gate / (1.0 + jnp.exp(-gate)) * lift).astype(BF16)

    def out_of_hidden(f, side):
        hs = hidden[f]

        def tile(step, carry):
            cols = pl.ds(pl.multiple_of(side * 2 * quarter + step * 512, 512), 512)
            part[f, :, :, :, cols] = mm(hs, wd[:, cols]).astype(BF16).reshape(DP // 2, 2, HALF, 512)
            return carry

        lax.fori_loop(0, 2 * quarter // 512, tile, 0)
        cols = (left, right)[side]
        send(
            part.at[f, :, oc, :, cols], core_in.at[f, :, :, cols],
            core_ss.at[f, side], core_rs.at[f, side], to_core,
        )

    def add_sibling(f, side):
        cols = (left, right)[side]
        ref = core_in.at[f, :, :, cols]
        remote(ref, ref, core_ss.at[f, side], core_rs.at[f, side], to_core).wait_recv()
        for p in (far_p, far_x, up_p, up_x, down_p, down_x, own_p, x_p):
            part[f, p, core, :, cols] = (
                part[f, p, core, :, cols].astype(F32) + core_in[f, p, :, cols].astype(F32)
            ).astype(BF16)

    def rs(f, i, p, cols, to):
        send(part.at[f, p, core, :, cols], sum_in.at[f, i, :, cols], rs_ss.at[f, i], rs_rs.at[f, i], to)

    def rs_value(f, i, cols):
        ref = sum_in.at[f, i, :, cols]
        remote(ref, ref, rs_ss.at[f, i], rs_rs.at[f, i], to_x).wait_recv()
        return ref[...].astype(F32)

    def add(f, i, p, cols):
        part[f, p, core, :, cols] = (
            part[f, p, core, :, cols].astype(F32) + rs_value(f, i, cols)
        ).astype(BF16)

    def first_left(f):
        add_sibling(f, 0)
        rs(f, 0, far_p, left, to_up)
        rs(f, 1, far_x, left, to_down)
        rs(f, 2, up_x, left, to_up)
        rs(f, 3, down_p, left, to_down)

    def first_right(f):
        add_sibling(f, 1)
        rs(f, 7, far_x, right, to_x)
        rs(f, 8, up_x, right, to_x)
        rs(f, 9, down_x, right, to_x)
        rs(f, 10, x_p, right, to_x)

    def relay_sums(f):
        add(f, 7, far_p, right)
        rs(f, 13, far_p, right_a, to_up)
        rs(f, 14, far_p, right_b, to_down)
        add(f, 0, up_p, left)
        rs(f, 4, up_p, left, to_up)
        add(f, 1, down_x, left)
        rs(f, 5, down_x, left, to_down)

    def relay_right(f):
        add(f, 8, up_p, right)
        add(f, 13, up_p, right_a)
        rs(f, 11, up_p, right, to_up)
        add(f, 9, down_p, right)
        add(f, 14, down_p, right_b)
        rs(f, 12, down_p, right, to_down)

    def relay_x(f):
        value = part[f, x_p, core, :, left].astype(F32) + rs_value(f, 2, left) + rs_value(f, 5, left)
        part[f, x_p, core, :, left] = value.astype(BF16)
        rs(f, 6, x_p, left, to_x)

    def whole_sums(f):
        value = part[f, own_p, core, :, right].astype(F32) + rs_value(f, 10, right)
        value = (value + rs_value(f, 11, right) + rs_value(f, 12, right)).astype(BF16).astype(F32)
        share = router_share()[f * HALF : (f + 1) * HALF]
        weighted[f, :, right] = (value * share).astype(BF16)
        value = part[f, own_p, core, :, left].astype(F32) + rs_value(f, 3, left) + rs_value(f, 4, left)
        value = (value + rs_value(f, 6, left)).astype(BF16).astype(F32)
        weighted[f, :, left] = (value * share).astype(BF16)
        to_rows = returned.at[pl.ds(pl.multiple_of(g * ROWS + f * HALF, HALF), HALF)]
        for k in range(1, GRP):
            q = (g + k) % GRP
            cols = pl.ds(pl.multiple_of(q * feats, feats), feats)
            send(weighted.at[f, :, cols], to_rows, ret_ss.at[f, k], ret_rs.at[f, k], (d, q))
        copy = pltpu.make_async_copy(weighted.at[f, :, mine_cols], to_rows, own_sem.at[2 + f])
        copy.start()
        own_rows.append(copy)

    share_of = []

    def router_share():
        if not share_of:
            own_logits.wait()
            for k in range(1, GRP):
                frm = (g - k + GRP) % GRP
                remote(logit_part.at[frm], logit_all.at[frm], log_ss.at[k], log_rs.at[k], (d, frm)).wait_recv()
            logits = logit_all[0]
            for q in range(1, GRP):
                logits = logits + logit_all[q]
            grown = jnp.exp(logits - jnp.max(logits, axis=1, keepdims=True))
            column = iota(logits.shape, 1) == g * (logits.shape[1] // GRP)
            picked = jnp.sum(jnp.where(column, grown, 0.0), axis=1, keepdims=True)
            share_of.append(picked / jnp.sum(grown, axis=1, keepdims=True))
        return share_of[0]

    own_out(0)
    relay_near(0)
    own_out(1)
    relay_left(0)
    relay_far(0)
    relay_near(1)
    last_near(0)
    relay_left(1)
    last_far(0)
    sibs(0)
    loads[2].wait()
    loads[3].wait()
    into_hidden(0,0)
    relay_far(1)
    into_hidden(0,1)
    last_near(1)
    loads[4].wait()
    out_of_hidden(0,1)
    out_of_hidden(0,0)
    first_right(0)
    first_left(0)
    last_far(1)
    for k in range(1, GRP):
        q = (g + k) % GRP
        send(logit_part.at[q], logit_all.at[g], log_ss.at[k], log_rs.at[k], (d, q))
    own_logits = pltpu.make_async_copy(logit_part.at[g], logit_all.at[g], own_sem.at[4])
    own_logits.start()
    index = index_ref[...].T
    top = jnp.floor(index * (1.0 / 128.0))
    high_ref[...] = top.astype(BF16)
    low_ref[...] = ones(index - top * 128.0 == iota(index.shape, 0, F32))
    sibs(1)
    into_hidden(1,0)
    relay_sums(0)
    into_hidden(1,1)
    relay_right(0)
    out_of_hidden(1,1)
    relay_x(0)
    out_of_hidden(1,0)
    first_right(1)
    first_left(1)
    whole_sums(0)
    relay_sums(1)
    relay_right(1)
    relay_x(1)
    whole_sums(1)
    own_rows[2].wait()
    own_rows[3].wait()
    for f in range(2):
        for k in range(1, GRP):
            frm = (g - k + GRP) % GRP
            frm_rows = returned.at[pl.ds(pl.multiple_of(frm * ROWS + f * HALF, HALF), HALF)]
            remote(frm_rows, frm_rows, ret_ss.at[f, k], ret_rs.at[f, k], (d, frm)).wait_recv()

    block_rows = returned[...]
    if quick:
        base = BLK
        kept_home = pltpu.make_async_copy(returned, back_ref.at[pl.ds(0, BLK)], own_sem.at[5])
        kept_home.start()
        back = lax.dot_general(
            spread[...], block_rows, (((0,), (0,)), ((), ())), preferred_element_type=F32
        )
    else:
        base = 0
        back = mm(spread[...], block_rows)
    outgoing[...] = back.astype(BF16).reshape(DP, cap, feats)
    to_rows = back_ref.at[pl.ds(pl.multiple_of(base + d * cap, 16), cap)]
    for k in range(1, DP):
        to = (d + k) % DP
        send(outgoing.at[to], to_rows, out_ss.at[k], out_rs.at[k], (to, g))
    own = pltpu.make_async_copy(outgoing.at[d], to_rows, own_sem.at[6])
    own.start()
    own.wait()
    if quick:
        kept_home.wait()
    for k in range(1, DP):
        frm = (d - k + DP) % DP
        frm_rows = back_ref.at[pl.ds(pl.multiple_of(base + frm * cap, 16), cap)]
        remote(outgoing.at[frm], frm_rows, out_ss.at[k], out_rs.at[k], (frm, g)).wait_recv()

    if not quick:
        for k in range(1, DP):
            to = (d + k) % DP
            remote(packed.at[to], arrived.at[d], tok_ss.at[k], tok_rs.at[k], (to, g)).wait_send()
    for copy in sent:
        copy.wait_send()


def mix_kernel(high, low, back, out_hbm, out, sem):
    tile = 512
    n_tile = out.shape[0] // tile
    rows = back.shape[0]

    def copy(t):
        at = pl.ds(pl.multiple_of(t * tile, tile), tile)
        return pltpu.make_async_copy(out.at[at], out_hbm.at[at], sem.at[t])

    def step(t, carry):
        parts = []
        for i in range(tile // 128):
            here = jnp.full((1, rows), jnp.asarray(t * (tile // 128) + i, jnp.int32).astype(F32)).astype(BF16)
            parts.append(jnp.where(high[...] == here, low[...], 0.0))
        at = pl.ds(pl.multiple_of(t * tile, tile), tile)
        out[at, :] = mm(jnp.concatenate(parts, axis=0), back[...]).astype(BF16)
        copy(t).start()
        return carry

    if rows > 1024:
        lax.fori_loop(0, n_tile, step, 0)
    else:
        for t in range(n_tile):
            step(t, 0)
    for t in range(n_tile):
        copy(t).wait()


def route(tokens, router_weight, gate_weight, up_weight, down_weight, picks, quick):
    cap = NEAR if quick else BLK
    packed = DP * cap
    n_back = packed + (BLK if quick else 0)
    tok_rows, feats = tokens.shape
    units, wide = down_weight.shape[1:]
    n_exp = router_weight.shape[1]
    dma = pltpu.SemaphoreType.DMA
    any_spec = pl.BlockSpec(memory_space=pl.ANY)
    vmem_spec = pl.BlockSpec(memory_space=pltpu.VMEM)
    return pl.pallas_call(
        functools.partial(expert_kernel, quick),
        out_shape=(
            jax.ShapeDtypeStruct((n_back, feats), BF16),
            jax.ShapeDtypeStruct((128, n_back), BF16),
            jax.ShapeDtypeStruct((128, n_back), BF16),
            jax.ShapeDtypeStruct((1, 1), F32),
        ),
        in_specs=[vmem_spec] + [any_spec] * 5,
        out_specs=(any_spec, vmem_spec, vmem_spec, pl.BlockSpec(memory_space=pltpu.SMEM)),
        scratch_shapes=[
            pltpu.VMEM((n_back, 128), F32),
            pltpu.VMEM((tok_rows, feats), BF16),
            pltpu.VMEM((feats, n_exp), F32),
            pltpu.VMEM((wide, units), BF16),
            pltpu.VMEM((wide, units), BF16),
            pltpu.VMEM((units, wide), BF16),
            pltpu.VMEM((BLK, tok_rows), BF16),
            pltpu.VMEM((DP, cap, feats), BF16),
            pltpu.VMEM((DP, cap, feats), BF16),
            pltpu.VMEM((BLK, packed) if quick else (packed, BLK), BF16),
            pltpu.VMEM((GRP, ROWS, feats), BF16),
            pltpu.VMEM((GRP, ROWS, n_exp), F32),
            pltpu.VMEM((GRP, ROWS, n_exp), F32),
            pltpu.VMEM((2, DP // 2, 2, HALF, wide), BF16),
            pltpu.VMEM((2, DP * HALF, units), BF16),
            pltpu.VMEM((2, DP // 2, 2, HALF, wide), BF16),
            pltpu.VMEM((2, DP // 2, HALF, wide), BF16),
            pltpu.VMEM((2, 15, HALF, wide), BF16),
            pltpu.VMEM((2, HALF, wide), BF16),
            pltpu.VMEM((BLK, feats), BF16),
            pltpu.VMEM((DP, cap, feats), BF16),
            dma((5,)),
            dma((7,)),
            dma((DP,)), dma((DP,)),
            dma((2, GRP)), dma((2, GRP)),
            dma((GRP,)), dma((GRP,)),
            dma((2, 15)), dma((2, 15)),
            dma((2, 16)), dma((2, 16)),
            dma((2, 2)), dma((2, 2)),
            dma((2, 15)), dma((2, 15)),
            dma((2, GRP)), dma((2, GRP)),
            dma((DP,)), dma((DP,)),
        ],
        compiler_params=pltpu.CompilerParams(
            collective_id=1 if quick else 2, has_side_effects=True, vmem_limit_bytes=60 * 2**20
        ),
        cost_estimate=pl.CostEstimate(
            flops=11 * 10**9, bytes_accessed=18 * 2**20, transcendentals=512 * 512
        ),
        name="experts" if quick else "experts_any",
    )(
        picks, tokens, router_weight, gate_weight[0], up_weight[0], down_weight[0]
    )


def mix(back, high, low, tok_rows):
    rows, feats = back.shape
    vmem_spec = pl.BlockSpec(memory_space=pltpu.VMEM)
    return pl.pallas_call(
        mix_kernel,
        out_shape=jax.ShapeDtypeStruct((tok_rows, feats), BF16),
        in_specs=[vmem_spec] * 3,
        out_specs=pl.BlockSpec(memory_space=pl.ANY),
        scratch_shapes=[pltpu.VMEM((tok_rows, feats), BF16), pltpu.SemaphoreType.DMA((tok_rows // 512,))],
        compiler_params=pltpu.CompilerParams(vmem_limit_bytes=60 * 2**20),
        cost_estimate=pl.CostEstimate(
            flops=2 * tok_rows * rows * feats, bytes_accessed=6 * 2**20, transcendentals=0
        ),
        name="mix",
    )(high, low, back)


def shards(tokens, router_weight, gate_weight, up_weight, down_weight, picks):
    tok_rows = tokens.shape[0]
    flight, capacity = picks.shape
    args = (tokens, router_weight, gate_weight, up_weight, down_weight)
    back, high, low, fit = route(*args, picks, True)

    def any_picks():
        blocks = picks.reshape(flight, DP, ROWS).transpose(1, 0, 2).reshape(DP, BLK)
        back, high, low, _ = route(*args, blocks, False)
        return mix(back, high, low, tok_rows)

    return lax.cond(fit[0, 0] <= NEAR, lambda: mix(back, high, low, tok_rows), any_picks)


def solution(mesh):
    in_specs = (
        P("dp", "group"),
        P("group", None),
        P("group", None, "dp"),
        P("group", None, "dp"),
        P("group", "dp", None),
        P(),
    )
    out_specs = P("dp", "group")
    return jax.shard_map(shards, mesh=mesh, in_specs=in_specs, out_specs=out_specs, check_vma=False)
```

```python
import functools

import jax
import jax.numpy as jnp
from jax import lax
from jax.experimental import pallas as pl
from jax.experimental.pallas import tpu as pltpu
from jax.sharding import PartitionSpec as P

MESH = pl.DeviceIdType.MESH
BF16 = jnp.bfloat16
F32 = jnp.float32
DP = 16
GRP = 8
NEAR = 16
BLK = 256
ROWS = 32
HALF = 16


def iota(shape, dim, dtype=jnp.int32):
    out = lax.broadcasted_iota(jnp.int32, shape, dim)
    return out if dtype == jnp.int32 else out.astype(dtype)


def earlier(n):
    return ones(iota((n, n), 0) < iota((n, n), 1))


def ones(mask):
    return jnp.where(mask, 1.0, 0.0).astype(BF16)


def mm(a, b):
    return jnp.dot(a, b, preferred_element_type=F32)


def over(values):
    return jnp.sum(values, axis=0, keepdims=True)


def best(hit, value):
    return jnp.max(jnp.where(hit, value, -1.0), axis=1, keepdims=True)


def fill_onehot(onehot, index):
    rows = index.shape[0]
    high = jnp.floor(index * (1.0 / 128.0))
    lane = iota((rows, 128), 1, F32)
    low = ones(index - high * 128.0 == lane)
    high = high.astype(BF16)
    for t in range(onehot.shape[1] // 128):
        onehot[:, t * 128 : (t + 1) * 128] = jnp.where(high == float(t), low, 0.0).astype(BF16)


def place_picks(picks_ref, me, tok_rows, index_ref, spread, fit_ref):
    flight, cap = picks_ref.shape
    n_pair = flight * DP
    tri = earlier(cap)
    picks = picks_ref[...]
    owner = picks // tok_rows
    local = (picks - owner * tok_rows).astype(F32)
    dev = iota((DP, cap), 0)
    dev_f = dev.astype(F32)
    at_me = dev == me
    owned = [ones(dev == owner[q : q + 1]) for q in range(flight)]
    stacked = jnp.concatenate(owned, axis=0)
    owned = [o.astype(F32) for o in owned]
    before = mm(stacked, tri)
    count = mm(stacked, jnp.full((cap, cap), 1.0, BF16))
    room = jnp.maximum(ROWS - count, 0.0)
    r, c = iota((n_pair, n_pair), 0), iota((n_pair, n_pair), 1)
    turn = 2 * (r // DP) + 1
    in_turn = (c + DP - turn % DP) % DP < (r + DP - turn % DP) % DP
    room_before = mm(ones((r // DP == c // DP) & in_turn), room.astype(BF16))
    earlier_expert = ones((r % DP == c % DP) & (c // DP < r // DP))

    def of(values, q):
        return values[q * DP : (q + 1) * DP]

    rank = [over(owned[q] * of(before, q)) for q in range(flight)]
    extra = [rank[q] >= ROWS for q in range(flight)]
    extra_no = mm(jnp.concatenate([ones(e) for e in extra], axis=0), tri)
    mine = [owner[q : q + 1] == me for q in range(flight)]
    sends, takes, to_me, fits = [], [], [], jnp.zeros((DP, DP), F32)
    for q in range(flight):
        no = extra_no[q : q + 1]
        first = of(room_before, q)
        dest = jnp.where(
            extra[q] & (no >= first) & (no < first + of(room, q)), 1.0, 0.0
        )
        to_me.append(over(jnp.where(at_me, dest, 0.0)))
        sends.append(jnp.where(mine[q], dest, 0.0).astype(BF16))
        takes.append((owned[q] * to_me[q]).astype(BF16))
        fits = fits + lax.dot_general(
            owned[q].astype(BF16), dest.astype(BF16), (((1,), (1,)), ((), ())),
            preferred_element_type=F32,
        )
    fit_ref[0, 0] = jnp.max(fits)

    def keys(hits):
        hits = jnp.concatenate(hits, axis=0)
        counts = mm(hits, jnp.full((cap, cap), 1.0, BF16)).astype(BF16)
        number = mm(hits, tri) + mm(earlier_expert, counts)
        hits = hits.astype(F32)
        return [over(of(hits, q) * (of(number, q) + NEAR * dev_f)) for q in range(flight)]

    n_far = DP * NEAR
    send_key, take_key = keys(sends), keys(takes)
    slot = iota((n_far, cap), 0, F32)
    far = jnp.full((n_far, cap), -1.0, F32)
    for q in range(flight):
        key = jnp.where(mine[q] & extra[q], send_key[q], -1.0)
        far = jnp.where(slot == key, local[q : q + 1], far)
    far = jnp.max(far, axis=1, keepdims=True)
    index_ref[pl.ds(BLK, n_far), :] = jnp.broadcast_to(far, (n_far, 128))
    slot = iota((ROWS, cap), 0, F32)
    column = iota((ROWS, n_far), 1, F32)
    for q in range(flight):
        key = jnp.where(mine[q], rank[q], -1.0)
        own = best(slot == key, local[q : q + 1])
        index_ref[pl.ds(q * ROWS, ROWS), :] = jnp.broadcast_to(own, (ROWS, 128))
        place = extra_no[q : q + 1] + over(
            jnp.where(at_me, of(count, q) - of(room_before, q), 0.0)
        )
        place = jnp.where(to_me[q] > 0.0, place, -1.0)
        source = best(slot == place, take_key[q])
        spread[pl.ds(q * ROWS, ROWS), :] = ones(source == column)


def expert_kernel(
    quick,
    picks_ref, tok_hbm, wr_hbm, wg_hbm, wu_hbm, wd_hbm,
    back_ref, high_ref, low_ref, fit_ref,
    index_ref, tok, wr, wg, wu, wd, onehot, packed, arrived, spread, rows, logit_part, logit_all,
    x, hidden, part, core_in, sum_in, weighted, returned, outgoing,
    load_sem, own_sem,
    tok_ss, tok_rs, row_ss, row_rs, log_ss, log_rs, ag_ss, ag_rs, sib_ss, sib_rs,
    core_ss, core_rs, rs_ss, rs_rs, ret_ss, ret_rs, out_ss, out_rs,
):
    cap = packed.shape[1]
    d, g = lax.axis_index("dp"), lax.axis_index("group")
    y, xl, core = d // 4, (d // 2) % 2, d % 2
    tok_rows = tok.shape[0]
    feats = tok.shape[1]

    def block(yy, xx, cc):
        return (yy * 2 + xx) * 2 + cc

    up, down, far = (y + 1) % 4, (y + 3) % 4, (y + 2) % 4
    ox, oc = 1 - xl, 1 - core
    to_up = (block(up, xl, core), g)
    to_down = (block(down, xl, core), g)
    to_x = (block(y, ox, core), g)
    to_core = (block(y, xl, oc), g)

    z, xh = g // 2, g % 2
    dp_moves, grp_moves = [], []
    for dy, dx, dc in sorted(
        ((dy, dx, dc) for dy in range(4) for dx in range(2) for dc in range(2)),
        key=lambda m: -(min(m[0], 4 - m[0]) + m[1]),
    ):
        if (dy, dx, dc) != (0, 0, 0):
            across = (xl + dx) % 2, (core + dc) % 2
            to, frm = block((y + dy) % 4, *across), block((y + 4 - dy) % 4, *across)
            dp_moves.append((len(dp_moves) + 1, to, frm))
    for dz, dx in sorted(
        ((dz, dx) for dz in range(4) for dx in range(2)), key=lambda m: -(min(m[0], 4 - m[0]) + 2 * m[1])
    ):
        if (dz, dx) != (0, 0):
            to, frm = (z + dz) % 4 * 2 + (xh + dx) % 2, (z + 4 - dz) % 4 * 2 + (xh + dx) % 2
            grp_moves.append((len(grp_moves) + 1, to, frm))

    sent = []

    def remote(src, dst, ss, rs, device):
        return pltpu.make_async_remote_copy(
            src_ref=src, dst_ref=dst, send_sem=ss, recv_sem=rs, device_id=device, device_id_type=MESH
        )

    def send(src, dst, ss, rs, device):
        copy = remote(src, dst, ss, rs, device)
        copy.start()
        sent.append(copy)
        return copy

    loads = []
    for i, (src, dst) in enumerate(
        ((tok_hbm, tok), (wr_hbm, wr), (wg_hbm, wg), (wu_hbm, wu), (wd_hbm, wd))
    ):
        copy = pltpu.make_async_copy(src, dst, load_sem.at[i])
        if i < 1:
            copy.start()
        loads.append(copy)

    barrier = pltpu.get_barrier_semaphore()
    for _, to, _ in dp_moves:
        pl.semaphore_signal(barrier, inc=1, device_id=(to, g), device_id_type=MESH)
    for _, to, _ in grp_moves:
        pl.semaphore_signal(barrier, inc=1, device_id=(d, to), device_id_type=MESH)

    if quick:
        place_picks(picks_ref, d, tok_rows, index_ref, spread, fit_ref)
    else:
        tri = earlier(BLK)
        local = picks_ref[...] - d * tok_rows
        mine = (local >= 0) & (local < tok_rows)
        rank = jnp.dot(
            jnp.where(mine, 1.0, 0.0).astype(BF16), tri, preferred_element_type=F32
        )
        rank = jnp.where(mine, rank, -1.0)
        local = local.astype(F32)
        slot_rank = iota((cap, BLK), 0, F32)
        for b in range(DP):
            chosen = jnp.where(slot_rank == rank[b : b + 1, :], local[b : b + 1, :], -1.0)
            index = jnp.max(chosen, axis=1, keepdims=True)
            index_ref[pl.ds(b * cap, cap), :] = jnp.broadcast_to(index, (cap, 128))

        owner = picks_ref[pl.ds(d, 1), :] // tok_rows
        is_owner = jnp.where(iota((DP, BLK), 0) == owner, 1.0, 0.0)
        ranks = jnp.dot(is_owner.astype(BF16), tri, preferred_element_type=F32)
        place = jnp.sum(is_owner * ranks, axis=0, keepdims=True) + owner.astype(F32) * cap
        spread[...] = jnp.where(iota((DP * cap, BLK), 0, F32) == place, 1.0, 0.0).astype(BF16)
        fit_ref[0, 0] = 0.0

    loads[0].wait()
    for copy in loads[1:]:
        copy.start()
    if quick:
        fill_onehot(onehot, index_ref[pl.ds(BLK, DP * cap), :])
        packed[...] = mm(onehot[...], tok[...]).astype(BF16).reshape(DP, cap, feats)
        pl.semaphore_wait(barrier, DP - 1 + GRP - 1)
        for k, to, _ in dp_moves:
            send(packed.at[to], arrived.at[d], tok_ss.at[k], tok_rs.at[k], (to, g))
        arrived[d] = jnp.zeros((cap, feats), BF16)
        fill_onehot(onehot, index_ref[pl.ds(0, BLK), :])
        kept = mm(onehot[...], tok[...])
    else:
        pl.semaphore_wait(barrier, DP - 1 + GRP - 1)

        def gather(step, carry):
            first = (d + 1 + step) % DP
            fill_onehot(onehot, index_ref[pl.ds(pl.multiple_of(first * cap, 16), cap), :])
            packed[first] = mm(onehot[...], tok[...]).astype(BF16)
            k = (first - d + DP) % DP

            @pl.when(first != d)
            def _():
                remote(packed.at[first], arrived.at[d], tok_ss.at[k], tok_rs.at[k], (first, g)).start()

            return carry

        lax.fori_loop(0, DP, gather, 0)
        own = pltpu.make_async_copy(packed.at[d], arrived.at[d], own_sem.at[6])
        own.start()
        own.wait()
    loads[1].wait()
    hi = wr[...].astype(BF16)
    lo = (wr[...] - hi.astype(F32)).astype(BF16)
    for k, frm in [(k, frm) for k, _, frm in dp_moves] if quick else [(k, (d - k + DP) % DP) for k in range(1, DP)]:
        remote(packed.at[frm], arrived.at[frm], tok_ss.at[k], tok_rs.at[k], (frm, g)).wait_recv()

    came = arrived[...].reshape(DP * cap, feats)
    if quick:
        taken = (mm(spread[...], came) + kept).astype(BF16)
    else:
        taken = lax.dot_general(
            spread[...], came, (((0,), (0,)), ((), ())), preferred_element_type=F32
        ).astype(BF16)
    rows[...] = taken.reshape(GRP, ROWS, feats)
    mine_cols = pl.ds(pl.multiple_of(g * feats, feats), feats)
    yx = y * 2 + xl

    def half_rows(f):
        return pl.ds(f * HALF, HALF)

    for f in range(2):
        for k, q, _ in grp_moves:
            send(
                rows.at[q, half_rows(f)], x.at[f, yx, core, :, mine_cols],
                row_ss.at[f, k], row_rs.at[f, k], (d, q),
            )
    own_rows = []
    for f in range(2):
        copy = pltpu.make_async_copy(
            rows.at[g, half_rows(f)], x.at[f, yx, core, :, mine_cols], own_sem.at[f]
        )
        copy.start()
        own_rows.append(copy)
    logits = mm(taken, hi) + mm(taken, lo)
    logit_part[...] = logits.reshape(GRP, ROWS, logits.shape[1])

    wide = x.shape[4]
    units = wg.shape[1]
    n_half = DP * HALF
    quarter = wide // 4
    left, right = pl.ds(0, 2 * quarter), pl.ds(2 * quarter, 2 * quarter)
    right_a, right_b = pl.ds(2 * quarter, quarter), pl.ds(3 * quarter, quarter)
    own_p, x_p = y * 2 + xl, y * 2 + ox
    up_p, down_p, far_p = up * 2 + xl, down * 2 + xl, far * 2 + xl
    up_x, down_x, far_x = up * 2 + ox, down * 2 + ox, far * 2 + ox
    at_place = (own_p, x_p, up_p, up_x, down_p, down_x, far_p, far_x)

    def ag(f, i, p, cols, to):
        ref = x.at[f, p, core, :, cols]
        send(ref, ref, ag_ss.at[f, i], ag_rs.at[f, i], to)

    def got(f, i, p, cols):
        ref = x.at[f, p, core, :, cols]
        remote(ref, ref, ag_ss.at[f, i], ag_rs.at[f, i], to_x).wait_recv()

    def sib(f, p, cols):
        i = [n for n in range(8) if at_place[n] is p][0] * 2 + (cols is right)
        ref = x.at[f, p, core, :, cols]
        send(ref, ref, sib_ss.at[f, i], sib_rs.at[f, i], to_core)

    def sibs(f):
        for i in range(16):
            ref = x.at[f, at_place[i // 2], oc, :, (left, right)[i % 2]]
            remote(ref, ref, sib_ss.at[f, i], sib_rs.at[f, i], to_core).wait_recv()

    def own_out(f):
        own_rows[f].wait()
        for k, _, frm in grp_moves:
            cols = pl.ds(pl.multiple_of(frm * feats, feats), feats)
            remote(
                rows.at[frm, half_rows(f)], x.at[f, yx, core, :, cols],
                row_ss.at[f, k], row_rs.at[f, k], (d, frm),
            ).wait_recv()
        ag(f, 0, own_p, left, to_x)
        ag(f, 7, own_p, right, to_up)
        ag(f, 8, own_p, right, to_down)
        ag(f, 1, own_p, left, to_up)
        ag(f, 2, own_p, left, to_down)
        ag(f, 9, own_p, right, to_x)
        sib(f, own_p, left)
        sib(f, own_p, right)

    def relay_near(f):
        got(f, 0, x_p, left)
        ag(f, 3, x_p, left, to_up)
        ag(f, 4, x_p, left, to_down)
        sib(f, x_p, left)
        got(f, 8, up_p, right)
        ag(f, 11, up_p, right_b, to_down)
        ag(f, 13, up_p, right, to_x)
        sib(f, up_p, right)
        got(f, 7, down_p, right)
        ag(f, 10, down_p, right_a, to_up)
        ag(f, 12, down_p, right, to_x)
        sib(f, down_p, right)

    def relay_left(f):
        got(f, 1, down_p, left)
        ag(f, 5, down_p, left, to_up)
        sib(f, down_p, left)
        got(f, 2, up_p, left)
        sib(f, up_p, left)
        got(f, 9, x_p, right)
        sib(f, x_p, right)

    def relay_far(f):
        got(f, 4, up_x, left)
        ag(f, 6, up_x, left, to_down)
        sib(f, up_x, left)
        got(f, 10, far_p, right_a)
        got(f, 11, far_p, right_b)
        ag(f, 14, far_p, right, to_x)
        sib(f, far_p, right)

    def last_near(f):
        got(f, 3, down_x, left)
        sib(f, down_x, left)
        got(f, 13, up_x, right)
        sib(f, up_x, right)
        got(f, 12, down_x, right)
        sib(f, down_x, right)

    def last_far(f):
        got(f, 5, far_p, left)
        sib(f, far_p, left)
        got(f, 6, far_x, left)
        sib(f, far_x, left)
        got(f, 14, far_x, right)
        sib(f, far_x, right)

    def into_hidden(f, step):
        cols = pl.ds(step * (units // 2), units // 2)
        xs = x[f].reshape(n_half, wide)
        gate = mm(xs, wg[:, cols])
        lift = mm(xs, wu[:, cols])
        hidden[f, :, cols] = (gate / (1.0 + jnp.exp(-gate)) * lift).astype(BF16)

    def out_of_hidden(f, side):
        hs = hidden[f]

        def tile(step, carry):
            cols = pl.ds(pl.multiple_of(side * 2 * quarter + step * 512, 512), 512)
            part[f, :, :, :, cols] = mm(hs, wd[:, cols]).astype(BF16).reshape(DP // 2, 2, HALF, 512)
            return carry

        lax.fori_loop(0, 2 * quarter // 512, tile, 0)
        cols = (left, right)[side]
        send(
            part.at[f, :, oc, :, cols], core_in.at[f, :, :, cols],
            core_ss.at[f, side], core_rs.at[f, side], to_core,
        )

    def add_sibling(f, side):
        cols = (left, right)[side]
        ref = core_in.at[f, :, :, cols]
        remote(ref, ref, core_ss.at[f, side], core_rs.at[f, side], to_core).wait_recv()
        for p in (far_p, far_x, up_p, up_x, down_p, down_x, own_p, x_p):
            part[f, p, core, :, cols] = (
                part[f, p, core, :, cols].astype(F32) + core_in[f, p, :, cols].astype(F32)
            ).astype(BF16)

    def rs(f, i, p, cols, to):
        send(part.at[f, p, core, :, cols], sum_in.at[f, i, :, cols], rs_ss.at[f, i], rs_rs.at[f, i], to)

    def rs_value(f, i, cols):
        ref = sum_in.at[f, i, :, cols]
        remote(ref, ref, rs_ss.at[f, i], rs_rs.at[f, i], to_x).wait_recv()
        return ref[...].astype(F32)

    def add(f, i, p, cols):
        part[f, p, core, :, cols] = (
            part[f, p, core, :, cols].astype(F32) + rs_value(f, i, cols)
        ).astype(BF16)

    def first_left(f):
        add_sibling(f, 0)
        rs(f, 0, far_p, left, to_up)
        rs(f, 1, far_x, left, to_down)
        rs(f, 2, up_x, left, to_up)
        rs(f, 3, down_p, left, to_down)

    def first_right(f):
        add_sibling(f, 1)
        rs(f, 7, far_x, right, to_x)
        rs(f, 8, up_x, right, to_x)
        rs(f, 9, down_x, right, to_x)
        rs(f, 10, x_p, right, to_x)

    def relay_sums(f):
        add(f, 7, far_p, right)
        rs(f, 13, far_p, right_a, to_up)
        rs(f, 14, far_p, right_b, to_down)
        add(f, 0, up_p, left)
        rs(f, 4, up_p, left, to_up)
        add(f, 1, down_x, left)
        rs(f, 5, down_x, left, to_down)

    def relay_right(f):
        add(f, 8, up_p, right)
        add(f, 13, up_p, right_a)
        rs(f, 11, up_p, right, to_up)
        add(f, 9, down_p, right)
        add(f, 14, down_p, right_b)
        rs(f, 12, down_p, right, to_down)

    def relay_x(f):
        value = part[f, x_p, core, :, left].astype(F32) + rs_value(f, 2, left) + rs_value(f, 5, left)
        part[f, x_p, core, :, left] = value.astype(BF16)
        rs(f, 6, x_p, left, to_x)

    def whole_sums(f):
        value = part[f, own_p, core, :, right].astype(F32) + rs_value(f, 10, right)
        value = (value + rs_value(f, 11, right) + rs_value(f, 12, right)).astype(BF16).astype(F32)
        share = router_share()[f * HALF : (f + 1) * HALF]
        weighted[f, :, right] = (value * share).astype(BF16)
        value = part[f, own_p, core, :, left].astype(F32) + rs_value(f, 3, left) + rs_value(f, 4, left)
        value = (value + rs_value(f, 6, left)).astype(BF16).astype(F32)
        weighted[f, :, left] = (value * share).astype(BF16)
        to_rows = returned.at[pl.ds(pl.multiple_of(g * ROWS + f * HALF, HALF), HALF)]
        for k, q, _ in grp_moves:
            cols = pl.ds(pl.multiple_of(q * feats, feats), feats)
            send(weighted.at[f, :, cols], to_rows, ret_ss.at[f, k], ret_rs.at[f, k], (d, q))
        copy = pltpu.make_async_copy(weighted.at[f, :, mine_cols], to_rows, own_sem.at[2 + f])
        copy.start()
        own_rows.append(copy)

    share_of = []

    def router_share():
        if not share_of:
            own_logits.wait()
            for k, _, frm in grp_moves:
                remote(logit_part.at[frm], logit_all.at[frm], log_ss.at[k], log_rs.at[k], (d, frm)).wait_recv()
            logits = logit_all[0]
            for q in range(1, GRP):
                logits = logits + logit_all[q]
            grown = jnp.exp(logits - jnp.max(logits, axis=1, keepdims=True))
            column = iota(logits.shape, 1) == g * (logits.shape[1] // GRP)
            picked = jnp.sum(jnp.where(column, grown, 0.0), axis=1, keepdims=True)
            share_of.append(picked / jnp.sum(grown, axis=1, keepdims=True))
        return share_of[0]

    own_out(0)
    relay_near(0)
    own_out(1)
    relay_left(0)
    relay_far(0)
    relay_near(1)
    last_near(0)
    relay_left(1)
    last_far(0)
    sibs(0)
    loads[2].wait()
    loads[3].wait()
    into_hidden(0,0)
    relay_far(1)
    into_hidden(0,1)
    last_near(1)
    loads[4].wait()
    out_of_hidden(0,1)
    out_of_hidden(0,0)
    first_right(0)
    first_left(0)
    last_far(1)
    for k, q, _ in grp_moves:
        send(logit_part.at[q], logit_all.at[g], log_ss.at[k], log_rs.at[k], (d, q))
    own_logits = pltpu.make_async_copy(logit_part.at[g], logit_all.at[g], own_sem.at[4])
    own_logits.start()
    index = index_ref[...].T
    top = jnp.floor(index * (1.0 / 128.0))
    high_ref[...] = top.astype(BF16)
    low_ref[...] = ones(index - top * 128.0 == iota(index.shape, 0, F32))
    sibs(1)
    into_hidden(1,0)
    relay_sums(0)
    into_hidden(1,1)
    relay_right(0)
    out_of_hidden(1,1)
    relay_x(0)
    out_of_hidden(1,0)
    first_right(1)
    first_left(1)
    whole_sums(0)
    relay_sums(1)
    relay_right(1)
    relay_x(1)
    whole_sums(1)
    own_rows[2].wait()
    own_rows[3].wait()
    for f in range(2):
        for k, _, frm in grp_moves:
            frm_rows = returned.at[pl.ds(pl.multiple_of(frm * ROWS + f * HALF, HALF), HALF)]
            remote(frm_rows, frm_rows, ret_ss.at[f, k], ret_rs.at[f, k], (d, frm)).wait_recv()

    block_rows = returned[...]
    if quick:
        base = BLK
        kept_home = pltpu.make_async_copy(returned, back_ref.at[pl.ds(0, BLK)], own_sem.at[5])
        kept_home.start()
        back = lax.dot_general(
            spread[...], block_rows, (((0,), (0,)), ((), ())), preferred_element_type=F32
        )
    else:
        base = 0
        back = mm(spread[...], block_rows)
    outgoing[...] = back.astype(BF16).reshape(DP, cap, feats)
    to_rows = back_ref.at[pl.ds(pl.multiple_of(base + d * cap, 16), cap)]
    for k, to, _ in dp_moves:
        send(outgoing.at[to], to_rows, out_ss.at[k], out_rs.at[k], (to, g))
    own = pltpu.make_async_copy(outgoing.at[d], to_rows, own_sem.at[6])
    own.start()
    own.wait()
    if quick:
        kept_home.wait()
    for k, _, frm in dp_moves:
        frm_rows = back_ref.at[pl.ds(pl.multiple_of(base + frm * cap, 16), cap)]
        remote(outgoing.at[frm], frm_rows, out_ss.at[k], out_rs.at[k], (frm, g)).wait_recv()

    if not quick:
        for k in range(1, DP):
            to = (d + k) % DP
            remote(packed.at[to], arrived.at[d], tok_ss.at[k], tok_rs.at[k], (to, g)).wait_send()
    for copy in sent:
        copy.wait_send()


def mix_kernel(high, low, back, out_hbm, out, sem):
    tile = 512
    n_tile = out.shape[0] // tile
    rows = back.shape[0]

    def copy(t):
        at = pl.ds(pl.multiple_of(t * tile, tile), tile)
        return pltpu.make_async_copy(out.at[at], out_hbm.at[at], sem.at[t])

    def step(t, carry):
        parts = []
        for i in range(tile // 128):
            here = jnp.full((1, rows), jnp.asarray(t * (tile // 128) + i, jnp.int32).astype(F32)).astype(BF16)
            parts.append(jnp.where(high[...] == here, low[...], 0.0))
        at = pl.ds(pl.multiple_of(t * tile, tile), tile)
        out[at, :] = mm(jnp.concatenate(parts, axis=0), back[...]).astype(BF16)
        copy(t).start()
        return carry

    if rows > 1024:
        lax.fori_loop(0, n_tile, step, 0)
    else:
        for t in range(n_tile):
            step(t, 0)
    for t in range(n_tile):
        copy(t).wait()


def route(tokens, router_weight, gate_weight, up_weight, down_weight, picks, quick):
    cap = NEAR if quick else BLK
    packed = DP * cap
    n_back = packed + (BLK if quick else 0)
    tok_rows, feats = tokens.shape
    units, wide = down_weight.shape[1:]
    n_exp = router_weight.shape[1]
    dma = pltpu.SemaphoreType.DMA
    any_spec = pl.BlockSpec(memory_space=pl.ANY)
    vmem_spec = pl.BlockSpec(memory_space=pltpu.VMEM)
    return pl.pallas_call(
        functools.partial(expert_kernel, quick),
        out_shape=(
            jax.ShapeDtypeStruct((n_back, feats), BF16),
            jax.ShapeDtypeStruct((128, n_back), BF16),
            jax.ShapeDtypeStruct((128, n_back), BF16),
            jax.ShapeDtypeStruct((1, 1), F32),
        ),
        in_specs=[vmem_spec] + [any_spec] * 5,
        out_specs=(any_spec, vmem_spec, vmem_spec, pl.BlockSpec(memory_space=pltpu.SMEM)),
        scratch_shapes=[
            pltpu.VMEM((n_back, 128), F32),
            pltpu.VMEM((tok_rows, feats), BF16),
            pltpu.VMEM((feats, n_exp), F32),
            pltpu.VMEM((wide, units), BF16),
            pltpu.VMEM((wide, units), BF16),
            pltpu.VMEM((units, wide), BF16),
            pltpu.VMEM((BLK, tok_rows), BF16),
            pltpu.VMEM((DP, cap, feats), BF16),
            pltpu.VMEM((DP, cap, feats), BF16),
            pltpu.VMEM((BLK, packed) if quick else (packed, BLK), BF16),
            pltpu.VMEM((GRP, ROWS, feats), BF16),
            pltpu.VMEM((GRP, ROWS, n_exp), F32),
            pltpu.VMEM((GRP, ROWS, n_exp), F32),
            pltpu.VMEM((2, DP // 2, 2, HALF, wide), BF16),
            pltpu.VMEM((2, DP * HALF, units), BF16),
            pltpu.VMEM((2, DP // 2, 2, HALF, wide), BF16),
            pltpu.VMEM((2, DP // 2, HALF, wide), BF16),
            pltpu.VMEM((2, 15, HALF, wide), BF16),
            pltpu.VMEM((2, HALF, wide), BF16),
            pltpu.VMEM((BLK, feats), BF16),
            pltpu.VMEM((DP, cap, feats), BF16),
            dma((5,)),
            dma((7,)),
            dma((DP,)), dma((DP,)),
            dma((2, GRP)), dma((2, GRP)),
            dma((GRP,)), dma((GRP,)),
            dma((2, 15)), dma((2, 15)),
            dma((2, 16)), dma((2, 16)),
            dma((2, 2)), dma((2, 2)),
            dma((2, 15)), dma((2, 15)),
            dma((2, GRP)), dma((2, GRP)),
            dma((DP,)), dma((DP,)),
        ],
        compiler_params=pltpu.CompilerParams(
            collective_id=1 if quick else 2, has_side_effects=True, vmem_limit_bytes=60 * 2**20
        ),
        cost_estimate=pl.CostEstimate(
            flops=11 * 10**9, bytes_accessed=18 * 2**20, transcendentals=512 * 512
        ),
        name="experts" if quick else "experts_any",
    )(
        picks, tokens, router_weight, gate_weight[0], up_weight[0], down_weight[0]
    )


def mix(back, high, low, tok_rows):
    rows, feats = back.shape
    vmem_spec = pl.BlockSpec(memory_space=pltpu.VMEM)
    return pl.pallas_call(
        mix_kernel,
        out_shape=jax.ShapeDtypeStruct((tok_rows, feats), BF16),
        in_specs=[vmem_spec] * 3,
        out_specs=pl.BlockSpec(memory_space=pl.ANY),
        scratch_shapes=[pltpu.VMEM((tok_rows, feats), BF16), pltpu.SemaphoreType.DMA((tok_rows // 512,))],
        compiler_params=pltpu.CompilerParams(vmem_limit_bytes=60 * 2**20),
        cost_estimate=pl.CostEstimate(
            flops=2 * tok_rows * rows * feats, bytes_accessed=6 * 2**20, transcendentals=0
        ),
        name="mix",
    )(high, low, back)


def shards(tokens, router_weight, gate_weight, up_weight, down_weight, picks):
    tok_rows = tokens.shape[0]
    flight, capacity = picks.shape
    args = (tokens, router_weight, gate_weight, up_weight, down_weight)
    back, high, low, fit = route(*args, picks, True)

    def any_picks():
        blocks = picks.reshape(flight, DP, ROWS).transpose(1, 0, 2).reshape(DP, BLK)
        back, high, low, _ = route(*args, blocks, False)
        return mix(back, high, low, tok_rows)

    return lax.cond(fit[0, 0] <= NEAR, lambda: mix(back, high, low, tok_rows), any_picks)


def solution(mesh):
    in_specs = (
        P("dp", "group"),
        P("group", None),
        P("group", None, "dp"),
        P("group", None, "dp"),
        P("group", "dp", None),
        P(),
    )
    out_specs = P("dp", "group")
    return jax.shard_map(shards, mesh=mesh, in_specs=in_specs, out_specs=out_specs, check_vma=False)
```

```python
import functools

import jax
import jax.numpy as jnp
from jax import lax
from jax.experimental import pallas as pl
from jax.experimental.pallas import tpu as pltpu
from jax.sharding import PartitionSpec as P

MESH = pl.DeviceIdType.MESH
BF16 = jnp.bfloat16
F32 = jnp.float32
DP = 16
GRP = 8
NEAR = 16
BLK = 256
ROWS = 32
HALF = 16


def iota(shape, dim, dtype=jnp.int32):
    out = lax.broadcasted_iota(jnp.int32, shape, dim)
    return out if dtype == jnp.int32 else out.astype(dtype)


def earlier(n):
    return ones(iota((n, n), 0) < iota((n, n), 1))


def ones(mask):
    return jnp.where(mask, 1.0, 0.0).astype(BF16)


def mm(a, b):
    return jnp.dot(a, b, preferred_element_type=F32)


def over(values):
    return jnp.sum(values, axis=0, keepdims=True)


def best(hit, value):
    return jnp.max(jnp.where(hit, value, -1.0), axis=1, keepdims=True)


def fill_onehot(onehot, index):
    rows = index.shape[0]
    high = jnp.floor(index * (1.0 / 128.0))
    lane = iota((rows, 128), 1, F32)
    low = ones(index - high * 128.0 == lane)
    high = high.astype(BF16)
    for t in range(onehot.shape[1] // 128):
        onehot[:, t * 128 : (t + 1) * 128] = jnp.where(high == float(t), low, 0.0).astype(BF16)


def place_picks(picks_ref, me, tok_rows, index_ref, spread, fit_ref):
    flight, cap = picks_ref.shape
    n_pair = flight * DP
    tri = earlier(cap)
    picks = picks_ref[...]
    owner = picks // tok_rows
    local = (picks - owner * tok_rows).astype(F32)
    dev = iota((DP, cap), 0)
    dev_f = dev.astype(F32)
    at_me = dev == me
    owned = [ones(dev == owner[q : q + 1]) for q in range(flight)]
    stacked = jnp.concatenate(owned, axis=0)
    owned = [o.astype(F32) for o in owned]
    before = mm(stacked, tri)
    count = mm(stacked, jnp.full((cap, cap), 1.0, BF16))
    room = jnp.maximum(ROWS - count, 0.0)
    r, c = iota((n_pair, n_pair), 0), iota((n_pair, n_pair), 1)
    turn = 2 * (r // DP) + 1
    in_turn = (c + DP - turn % DP) % DP < (r + DP - turn % DP) % DP
    room_before = mm(ones((r // DP == c // DP) & in_turn), room.astype(BF16))
    earlier_expert = ones((r % DP == c % DP) & (c // DP < r // DP))

    def of(values, q):
        return values[q * DP : (q + 1) * DP]

    rank = [over(owned[q] * of(before, q)) for q in range(flight)]
    extra = [rank[q] >= ROWS for q in range(flight)]
    extra_no = mm(jnp.concatenate([ones(e) for e in extra], axis=0), tri)
    mine = [owner[q : q + 1] == me for q in range(flight)]
    sends, takes, to_me, fits = [], [], [], jnp.zeros((DP, DP), F32)
    for q in range(flight):
        no = extra_no[q : q + 1]
        first = of(room_before, q)
        dest = jnp.where(
            extra[q] & (no >= first) & (no < first + of(room, q)), 1.0, 0.0
        )
        to_me.append(over(jnp.where(at_me, dest, 0.0)))
        sends.append(jnp.where(mine[q], dest, 0.0).astype(BF16))
        takes.append((owned[q] * to_me[q]).astype(BF16))
        fits = fits + lax.dot_general(
            owned[q].astype(BF16), dest.astype(BF16), (((1,), (1,)), ((), ())),
            preferred_element_type=F32,
        )
    fit_ref[0, 0] = jnp.max(fits)

    def keys(hits):
        hits = jnp.concatenate(hits, axis=0)
        counts = mm(hits, jnp.full((cap, cap), 1.0, BF16)).astype(BF16)
        number = mm(hits, tri) + mm(earlier_expert, counts)
        hits = hits.astype(F32)
        return [over(of(hits, q) * (of(number, q) + NEAR * dev_f)) for q in range(flight)]

    n_far = DP * NEAR
    send_key, take_key = keys(sends), keys(takes)
    slot = iota((n_far, cap), 0, F32)
    far = jnp.full((n_far, cap), -1.0, F32)
    for q in range(flight):
        key = jnp.where(mine[q] & extra[q], send_key[q], -1.0)
        far = jnp.where(slot == key, local[q : q + 1], far)
    far = jnp.max(far, axis=1, keepdims=True)
    index_ref[pl.ds(BLK, n_far), :] = jnp.broadcast_to(far, (n_far, 128))
    slot = iota((ROWS, cap), 0, F32)
    column = iota((ROWS, n_far), 1, F32)
    for q in range(flight):
        key = jnp.where(mine[q], rank[q], -1.0)
        own = best(slot == key, local[q : q + 1])
        index_ref[pl.ds(q * ROWS, ROWS), :] = jnp.broadcast_to(own, (ROWS, 128))
        place = extra_no[q : q + 1] + over(
            jnp.where(at_me, of(count, q) - of(room_before, q), 0.0)
        )
        place = jnp.where(to_me[q] > 0.0, place, -1.0)
        source = best(slot == place, take_key[q])
        spread[pl.ds(q * ROWS, ROWS), :] = ones(source == column)


def expert_kernel(
    quick,
    picks_ref, tok_hbm, wr_hbm, wg_hbm, wu_hbm, wd_hbm,
    back_ref, high_ref, low_ref, fit_ref,
    index_ref, tok, wr, wg, wu, wd, onehot, packed, arrived, spread, rows, logit_part, logit_all,
    x, hidden, part, core_in, sum_in, weighted, returned, outgoing,
    load_sem, own_sem,
    tok_ss, tok_rs, row_ss, row_rs, log_ss, log_rs, ag_ss, ag_rs, sib_ss, sib_rs,
    core_ss, core_rs, rs_ss, rs_rs, ret_ss, ret_rs, out_ss, out_rs,
):
    cap = packed.shape[1]
    d, g = lax.axis_index("dp"), lax.axis_index("group")
    y, xl, core = d // 4, (d // 2) % 2, d % 2
    tok_rows = tok.shape[0]
    feats = tok.shape[1]

    def block(yy, xx, cc):
        return (yy * 2 + xx) * 2 + cc

    up, down, far = (y + 1) % 4, (y + 3) % 4, (y + 2) % 4
    ox, oc = 1 - xl, 1 - core
    to_up = (block(up, xl, core), g)
    to_down = (block(down, xl, core), g)
    to_x = (block(y, ox, core), g)
    to_core = (block(y, xl, oc), g)

    z, xh = g // 2, g % 2
    dp_moves, grp_moves = [], []
    for dy, dx, dc in sorted(
        ((dy, dx, dc) for dy in range(4) for dx in range(2) for dc in range(2)),
        key=lambda m: -(min(m[0], 4 - m[0]) + m[1]),
    ):
        if (dy, dx, dc) != (0, 0, 0):
            across = (xl + dx) % 2, (core + dc) % 2
            to, frm = block((y + dy) % 4, *across), block((y + 4 - dy) % 4, *across)
            dp_moves.append((len(dp_moves) + 1, to, frm))
    for dz, dx in sorted(
        ((dz, dx) for dz in range(4) for dx in range(2)), key=lambda m: -(min(m[0], 4 - m[0]) + 2 * m[1])
    ):
        if (dz, dx) != (0, 0):
            to, frm = (z + dz) % 4 * 2 + (xh + dx) % 2, (z + 4 - dz) % 4 * 2 + (xh + dx) % 2
            grp_moves.append((len(grp_moves) + 1, to, frm))

    sent = []

    def remote(src, dst, ss, rs, device):
        return pltpu.make_async_remote_copy(
            src_ref=src, dst_ref=dst, send_sem=ss, recv_sem=rs, device_id=device, device_id_type=MESH
        )

    def send(src, dst, ss, rs, device):
        copy = remote(src, dst, ss, rs, device)
        copy.start()
        sent.append(copy)
        return copy

    loads = []
    for i, (src, dst) in enumerate(
        ((tok_hbm, tok), (wr_hbm, wr), (wg_hbm, wg), (wu_hbm, wu), (wd_hbm, wd))
    ):
        copy = pltpu.make_async_copy(src, dst, load_sem.at[i])
        if i < 1:
            copy.start()
        loads.append(copy)

    barrier = pltpu.get_barrier_semaphore()
    for _, to, _ in dp_moves:
        pl.semaphore_signal(barrier, inc=1, device_id=(to, g), device_id_type=MESH)
    for _, to, _ in grp_moves:
        pl.semaphore_signal(barrier, inc=1, device_id=(d, to), device_id_type=MESH)

    if quick:
        place_picks(picks_ref, d, tok_rows, index_ref, spread, fit_ref)
    else:
        tri = earlier(BLK)
        local = picks_ref[...] - d * tok_rows
        mine = (local >= 0) & (local < tok_rows)
        rank = jnp.dot(
            jnp.where(mine, 1.0, 0.0).astype(BF16), tri, preferred_element_type=F32
        )
        rank = jnp.where(mine, rank, -1.0)
        local = local.astype(F32)
        slot_rank = iota((cap, BLK), 0, F32)
        for b in range(DP):
            chosen = jnp.where(slot_rank == rank[b : b + 1, :], local[b : b + 1, :], -1.0)
            index = jnp.max(chosen, axis=1, keepdims=True)
            index_ref[pl.ds(b * cap, cap), :] = jnp.broadcast_to(index, (cap, 128))

        owner = picks_ref[pl.ds(d, 1), :] // tok_rows
        is_owner = jnp.where(iota((DP, BLK), 0) == owner, 1.0, 0.0)
        ranks = jnp.dot(is_owner.astype(BF16), tri, preferred_element_type=F32)
        place = jnp.sum(is_owner * ranks, axis=0, keepdims=True) + owner.astype(F32) * cap
        spread[...] = jnp.where(iota((DP * cap, BLK), 0, F32) == place, 1.0, 0.0).astype(BF16)
        fit_ref[0, 0] = 0.0

    if quick:
        fill_onehot(onehot, index_ref[pl.ds(BLK, DP * cap), :])
    loads[0].wait()
    for copy in loads[1:]:
        copy.start()
    if quick:
        packed[...] = mm(onehot[...], tok[...]).astype(BF16).reshape(DP, cap, feats)
        pl.semaphore_wait(barrier, DP - 1 + GRP - 1)
        for k, to, _ in dp_moves:
            send(packed.at[to], arrived.at[d], tok_ss.at[k], tok_rs.at[k], (to, g))
        arrived[d] = jnp.zeros((cap, feats), BF16)
        fill_onehot(onehot, index_ref[pl.ds(0, BLK), :])
        kept = mm(onehot[...], tok[...])
    else:
        pl.semaphore_wait(barrier, DP - 1 + GRP - 1)

        def gather(step, carry):
            first = (d + 1 + step) % DP
            fill_onehot(onehot, index_ref[pl.ds(pl.multiple_of(first * cap, 16), cap), :])
            packed[first] = mm(onehot[...], tok[...]).astype(BF16)
            k = (first - d + DP) % DP

            @pl.when(first != d)
            def _():
                remote(packed.at[first], arrived.at[d], tok_ss.at[k], tok_rs.at[k], (first, g)).start()

            return carry

        lax.fori_loop(0, DP, gather, 0)
        own = pltpu.make_async_copy(packed.at[d], arrived.at[d], own_sem.at[6])
        own.start()
        own.wait()
    loads[1].wait()
    hi = wr[...].astype(BF16)
    lo = (wr[...] - hi.astype(F32)).astype(BF16)
    for k, frm in [(k, frm) for k, _, frm in dp_moves] if quick else [(k, (d - k + DP) % DP) for k in range(1, DP)]:
        remote(packed.at[frm], arrived.at[frm], tok_ss.at[k], tok_rs.at[k], (frm, g)).wait_recv()

    came = arrived[...].reshape(DP * cap, feats)
    if quick:
        taken = (mm(spread[...], came) + kept).astype(BF16)
    else:
        taken = lax.dot_general(
            spread[...], came, (((0,), (0,)), ((), ())), preferred_element_type=F32
        ).astype(BF16)
    rows[...] = taken.reshape(GRP, ROWS, feats)
    mine_cols = pl.ds(pl.multiple_of(g * feats, feats), feats)
    yx = y * 2 + xl

    def half_rows(f):
        return pl.ds(f * HALF, HALF)

    for f in range(2):
        for k, q, _ in grp_moves:
            send(
                rows.at[q, half_rows(f)], x.at[f, yx, core, :, mine_cols],
                row_ss.at[f, k], row_rs.at[f, k], (d, q),
            )
    own_rows = []
    for f in range(2):
        copy = pltpu.make_async_copy(
            rows.at[g, half_rows(f)], x.at[f, yx, core, :, mine_cols], own_sem.at[f]
        )
        copy.start()
        own_rows.append(copy)
    logits = mm(taken, hi) + mm(taken, lo)
    logit_part[...] = logits.reshape(GRP, ROWS, logits.shape[1])

    wide = x.shape[4]
    units = wg.shape[1]
    n_half = DP * HALF
    quarter = wide // 4
    left, right = pl.ds(0, 2 * quarter), pl.ds(2 * quarter, 2 * quarter)
    right_a, right_b = pl.ds(2 * quarter, quarter), pl.ds(3 * quarter, quarter)
    own_p, x_p = y * 2 + xl, y * 2 + ox
    up_p, down_p, far_p = up * 2 + xl, down * 2 + xl, far * 2 + xl
    up_x, down_x, far_x = up * 2 + ox, down * 2 + ox, far * 2 + ox
    at_place = (own_p, x_p, up_p, up_x, down_p, down_x, far_p, far_x)

    def ag(f, i, p, cols, to):
        ref = x.at[f, p, core, :, cols]
        send(ref, ref, ag_ss.at[f, i], ag_rs.at[f, i], to)

    def got(f, i, p, cols):
        ref = x.at[f, p, core, :, cols]
        remote(ref, ref, ag_ss.at[f, i], ag_rs.at[f, i], to_x).wait_recv()

    def sib(f, p, cols):
        i = [n for n in range(8) if at_place[n] is p][0] * 2 + (cols is right)
        ref = x.at[f, p, core, :, cols]
        send(ref, ref, sib_ss.at[f, i], sib_rs.at[f, i], to_core)

    def sibs(f):
        for i in range(16):
            ref = x.at[f, at_place[i // 2], oc, :, (left, right)[i % 2]]
            remote(ref, ref, sib_ss.at[f, i], sib_rs.at[f, i], to_core).wait_recv()

    def own_out(f):
        own_rows[f].wait()
        for k, _, frm in grp_moves:
            cols = pl.ds(pl.multiple_of(frm * feats, feats), feats)
            remote(
                rows.at[frm, half_rows(f)], x.at[f, yx, core, :, cols],
                row_ss.at[f, k], row_rs.at[f, k], (d, frm),
            ).wait_recv()
        ag(f, 0, own_p, left, to_x)
        ag(f, 7, own_p, right, to_up)
        ag(f, 8, own_p, right, to_down)
        ag(f, 1, own_p, left, to_up)
        ag(f, 2, own_p, left, to_down)
        ag(f, 9, own_p, right, to_x)
        sib(f, own_p, left)
        sib(f, own_p, right)

    def relay_near(f):
        got(f, 0, x_p, left)
        ag(f, 3, x_p, left, to_up)
        ag(f, 4, x_p, left, to_down)
        sib(f, x_p, left)
        got(f, 8, up_p, right)
        ag(f, 11, up_p, right_b, to_down)
        ag(f, 13, up_p, right, to_x)
        sib(f, up_p, right)
        got(f, 7, down_p, right)
        ag(f, 10, down_p, right_a, to_up)
        ag(f, 12, down_p, right, to_x)
        sib(f, down_p, right)

    def relay_left(f):
        got(f, 1, down_p, left)
        ag(f, 5, down_p, left, to_up)
        sib(f, down_p, left)
        got(f, 2, up_p, left)
        sib(f, up_p, left)
        got(f, 9, x_p, right)
        sib(f, x_p, right)

    def relay_far(f):
        got(f, 4, up_x, left)
        ag(f, 6, up_x, left, to_down)
        sib(f, up_x, left)
        got(f, 10, far_p, right_a)
        got(f, 11, far_p, right_b)
        ag(f, 14, far_p, right, to_x)
        sib(f, far_p, right)

    def last_near(f):
        got(f, 3, down_x, left)
        sib(f, down_x, left)
        got(f, 13, up_x, right)
        sib(f, up_x, right)
        got(f, 12, down_x, right)
        sib(f, down_x, right)

    def last_far(f):
        got(f, 5, far_p, left)
        sib(f, far_p, left)
        got(f, 6, far_x, left)
        sib(f, far_x, left)
        got(f, 14, far_x, right)
        sib(f, far_x, right)

    def into_hidden(f, step):
        cols = pl.ds(step * (units // 2), units // 2)
        xs = x[f].reshape(n_half, wide)
        gate = mm(xs, wg[:, cols])
        lift = mm(xs, wu[:, cols])
        hidden[f, :, cols] = (gate / (1.0 + jnp.exp(-gate)) * lift).astype(BF16)

    def out_of_hidden(f, side):
        hs = hidden[f]

        def tile(step, carry):
            cols = pl.ds(pl.multiple_of(side * 2 * quarter + step * 512, 512), 512)
            part[f, :, :, :, cols] = mm(hs, wd[:, cols]).astype(BF16).reshape(DP // 2, 2, HALF, 512)
            return carry

        lax.fori_loop(0, 2 * quarter // 512, tile, 0)
        cols = (left, right)[side]
        send(
            part.at[f, :, oc, :, cols], core_in.at[f, :, :, cols],
            core_ss.at[f, side], core_rs.at[f, side], to_core,
        )

    def add_sibling(f, side):
        cols = (left, right)[side]
        ref = core_in.at[f, :, :, cols]
        remote(ref, ref, core_ss.at[f, side], core_rs.at[f, side], to_core).wait_recv()
        for p in (far_p, far_x, up_p, up_x, down_p, down_x, own_p, x_p):
            part[f, p, core, :, cols] = (
                part[f, p, core, :, cols].astype(F32) + core_in[f, p, :, cols].astype(F32)
            ).astype(BF16)

    def rs(f, i, p, cols, to):
        send(part.at[f, p, core, :, cols], sum_in.at[f, i, :, cols], rs_ss.at[f, i], rs_rs.at[f, i], to)

    def rs_value(f, i, cols):
        ref = sum_in.at[f, i, :, cols]
        remote(ref, ref, rs_ss.at[f, i], rs_rs.at[f, i], to_x).wait_recv()
        return ref[...].astype(F32)

    def add(f, i, p, cols):
        part[f, p, core, :, cols] = (
            part[f, p, core, :, cols].astype(F32) + rs_value(f, i, cols)
        ).astype(BF16)

    def first_left(f):
        add_sibling(f, 0)
        rs(f, 0, far_p, left, to_up)
        rs(f, 1, far_x, left, to_down)
        rs(f, 2, up_x, left, to_up)
        rs(f, 3, down_p, left, to_down)

    def first_right(f):
        add_sibling(f, 1)
        rs(f, 7, far_x, right, to_x)
        rs(f, 8, up_x, right, to_x)
        rs(f, 9, down_x, right, to_x)
        rs(f, 10, x_p, right, to_x)

    def relay_sums(f):
        add(f, 7, far_p, right)
        rs(f, 13, far_p, right_a, to_up)
        rs(f, 14, far_p, right_b, to_down)
        add(f, 0, up_p, left)
        rs(f, 4, up_p, left, to_up)
        add(f, 1, down_x, left)
        rs(f, 5, down_x, left, to_down)

    def relay_right(f):
        add(f, 8, up_p, right)
        add(f, 13, up_p, right_a)
        rs(f, 11, up_p, right, to_up)
        add(f, 9, down_p, right)
        add(f, 14, down_p, right_b)
        rs(f, 12, down_p, right, to_down)

    def relay_x(f):
        value = part[f, x_p, core, :, left].astype(F32) + rs_value(f, 2, left) + rs_value(f, 5, left)
        part[f, x_p, core, :, left] = value.astype(BF16)
        rs(f, 6, x_p, left, to_x)

    def whole_sums(f):
        value = part[f, own_p, core, :, right].astype(F32) + rs_value(f, 10, right)
        value = (value + rs_value(f, 11, right) + rs_value(f, 12, right)).astype(BF16).astype(F32)
        share = router_share()[f * HALF : (f + 1) * HALF]
        weighted[f, :, right] = (value * share).astype(BF16)
        value = part[f, own_p, core, :, left].astype(F32) + rs_value(f, 3, left) + rs_value(f, 4, left)
        value = (value + rs_value(f, 6, left)).astype(BF16).astype(F32)
        weighted[f, :, left] = (value * share).astype(BF16)
        to_rows = returned.at[pl.ds(pl.multiple_of(g * ROWS + f * HALF, HALF), HALF)]
        for k, q, _ in grp_moves:
            cols = pl.ds(pl.multiple_of(q * feats, feats), feats)
            send(weighted.at[f, :, cols], to_rows, ret_ss.at[f, k], ret_rs.at[f, k], (d, q))
        copy = pltpu.make_async_copy(weighted.at[f, :, mine_cols], to_rows, own_sem.at[2 + f])
        copy.start()
        own_rows.append(copy)

    share_of = []

    def router_share():
        if not share_of:
            own_logits.wait()
            for k, _, frm in grp_moves:
                remote(logit_part.at[frm], logit_all.at[frm], log_ss.at[k], log_rs.at[k], (d, frm)).wait_recv()
            logits = logit_all[0]
            for q in range(1, GRP):
                logits = logits + logit_all[q]
            grown = jnp.exp(logits - jnp.max(logits, axis=1, keepdims=True))
            column = iota(logits.shape, 1) == g * (logits.shape[1] // GRP)
            picked = jnp.sum(jnp.where(column, grown, 0.0), axis=1, keepdims=True)
            share_of.append(picked / jnp.sum(grown, axis=1, keepdims=True))
        return share_of[0]

    own_out(0)
    relay_near(0)
    own_out(1)
    relay_left(0)
    relay_far(0)
    relay_near(1)
    last_near(0)
    relay_left(1)
    last_far(0)
    sibs(0)
    loads[2].wait()
    loads[3].wait()
    into_hidden(0,0)
    relay_far(1)
    into_hidden(0,1)
    last_near(1)
    loads[4].wait()
    out_of_hidden(0,1)
    out_of_hidden(0,0)
    first_right(0)
    first_left(0)
    last_far(1)
    for k, q, _ in grp_moves:
        send(logit_part.at[q], logit_all.at[g], log_ss.at[k], log_rs.at[k], (d, q))
    own_logits = pltpu.make_async_copy(logit_part.at[g], logit_all.at[g], own_sem.at[4])
    own_logits.start()
    index = index_ref[...].T
    top = jnp.floor(index * (1.0 / 128.0))
    high_ref[...] = top.astype(BF16)
    low_ref[...] = ones(index - top * 128.0 == iota(index.shape, 0, F32))
    sibs(1)
    into_hidden(1,0)
    relay_sums(0)
    into_hidden(1,1)
    relay_right(0)
    out_of_hidden(1,1)
    relay_x(0)
    out_of_hidden(1,0)
    first_right(1)
    first_left(1)
    whole_sums(0)
    relay_sums(1)
    relay_right(1)
    relay_x(1)
    whole_sums(1)
    own_rows[2].wait()
    own_rows[3].wait()
    for f in range(2):
        for k, _, frm in grp_moves:
            frm_rows = returned.at[pl.ds(pl.multiple_of(frm * ROWS + f * HALF, HALF), HALF)]
            remote(frm_rows, frm_rows, ret_ss.at[f, k], ret_rs.at[f, k], (d, frm)).wait_recv()

    block_rows = returned[...]
    if quick:
        base = BLK
        kept_home = pltpu.make_async_copy(returned, back_ref.at[pl.ds(0, BLK)], own_sem.at[5])
        kept_home.start()
        back = lax.dot_general(
            spread[...], block_rows, (((0,), (0,)), ((), ())), preferred_element_type=F32
        )
    else:
        base = 0
        back = mm(spread[...], block_rows)
    outgoing[...] = back.astype(BF16).reshape(DP, cap, feats)
    to_rows = back_ref.at[pl.ds(pl.multiple_of(base + d * cap, 16), cap)]
    for k, to, _ in dp_moves:
        send(outgoing.at[to], to_rows, out_ss.at[k], out_rs.at[k], (to, g))
    own = pltpu.make_async_copy(outgoing.at[d], to_rows, own_sem.at[6])
    own.start()
    own.wait()
    if quick:
        kept_home.wait()
    for k, _, frm in dp_moves:
        frm_rows = back_ref.at[pl.ds(pl.multiple_of(base + frm * cap, 16), cap)]
        remote(outgoing.at[frm], frm_rows, out_ss.at[k], out_rs.at[k], (frm, g)).wait_recv()

    if not quick:
        for k in range(1, DP):
            to = (d + k) % DP
            remote(packed.at[to], arrived.at[d], tok_ss.at[k], tok_rs.at[k], (to, g)).wait_send()
    for copy in sent:
        copy.wait_send()


def mix_kernel(high, low, back, out_hbm, out, sem):
    tile = 512
    n_tile = out.shape[0] // tile
    rows = back.shape[0]

    def copy(t):
        at = pl.ds(pl.multiple_of(t * tile, tile), tile)
        return pltpu.make_async_copy(out.at[at], out_hbm.at[at], sem.at[t])

    def step(t, carry):
        parts = []
        for i in range(tile // 128):
            here = jnp.full((1, rows), jnp.asarray(t * (tile // 128) + i, jnp.int32).astype(F32)).astype(BF16)
            parts.append(jnp.where(high[...] == here, low[...], 0.0))
        at = pl.ds(pl.multiple_of(t * tile, tile), tile)
        out[at, :] = mm(jnp.concatenate(parts, axis=0), back[...]).astype(BF16)
        copy(t).start()
        return carry

    if rows > 1024:
        lax.fori_loop(0, n_tile, step, 0)
    else:
        for t in range(n_tile):
            step(t, 0)
    for t in range(n_tile):
        copy(t).wait()


def route(tokens, router_weight, gate_weight, up_weight, down_weight, picks, quick):
    cap = NEAR if quick else BLK
    packed = DP * cap
    n_back = packed + (BLK if quick else 0)
    tok_rows, feats = tokens.shape
    units, wide = down_weight.shape[1:]
    n_exp = router_weight.shape[1]
    dma = pltpu.SemaphoreType.DMA
    any_spec = pl.BlockSpec(memory_space=pl.ANY)
    vmem_spec = pl.BlockSpec(memory_space=pltpu.VMEM)
    return pl.pallas_call(
        functools.partial(expert_kernel, quick),
        out_shape=(
            jax.ShapeDtypeStruct((n_back, feats), BF16),
            jax.ShapeDtypeStruct((128, n_back), BF16),
            jax.ShapeDtypeStruct((128, n_back), BF16),
            jax.ShapeDtypeStruct((1, 1), F32),
        ),
        in_specs=[vmem_spec] + [any_spec] * 5,
        out_specs=(any_spec, vmem_spec, vmem_spec, pl.BlockSpec(memory_space=pltpu.SMEM)),
        scratch_shapes=[
            pltpu.VMEM((n_back, 128), F32),
            pltpu.VMEM((tok_rows, feats), BF16),
            pltpu.VMEM((feats, n_exp), F32),
            pltpu.VMEM((wide, units), BF16),
            pltpu.VMEM((wide, units), BF16),
            pltpu.VMEM((units, wide), BF16),
            pltpu.VMEM((BLK, tok_rows), BF16),
            pltpu.VMEM((DP, cap, feats), BF16),
            pltpu.VMEM((DP, cap, feats), BF16),
            pltpu.VMEM((BLK, packed) if quick else (packed, BLK), BF16),
            pltpu.VMEM((GRP, ROWS, feats), BF16),
            pltpu.VMEM((GRP, ROWS, n_exp), F32),
            pltpu.VMEM((GRP, ROWS, n_exp), F32),
            pltpu.VMEM((2, DP // 2, 2, HALF, wide), BF16),
            pltpu.VMEM((2, DP * HALF, units), BF16),
            pltpu.VMEM((2, DP // 2, 2, HALF, wide), BF16),
            pltpu.VMEM((2, DP // 2, HALF, wide), BF16),
            pltpu.VMEM((2, 15, HALF, wide), BF16),
            pltpu.VMEM((2, HALF, wide), BF16),
            pltpu.VMEM((BLK, feats), BF16),
            pltpu.VMEM((DP, cap, feats), BF16),
            dma((5,)),
            dma((7,)),
            dma((DP,)), dma((DP,)),
            dma((2, GRP)), dma((2, GRP)),
            dma((GRP,)), dma((GRP,)),
            dma((2, 15)), dma((2, 15)),
            dma((2, 16)), dma((2, 16)),
            dma((2, 2)), dma((2, 2)),
            dma((2, 15)), dma((2, 15)),
            dma((2, GRP)), dma((2, GRP)),
            dma((DP,)), dma((DP,)),
        ],
        compiler_params=pltpu.CompilerParams(
            collective_id=1 if quick else 2, has_side_effects=True, vmem_limit_bytes=60 * 2**20
        ),
        cost_estimate=pl.CostEstimate(
            flops=11 * 10**9, bytes_accessed=18 * 2**20, transcendentals=512 * 512
        ),
        name="experts" if quick else "experts_any",
    )(
        picks, tokens, router_weight, gate_weight[0], up_weight[0], down_weight[0]
    )


def mix(back, high, low, tok_rows):
    rows, feats = back.shape
    vmem_spec = pl.BlockSpec(memory_space=pltpu.VMEM)
    return pl.pallas_call(
        mix_kernel,
        out_shape=jax.ShapeDtypeStruct((tok_rows, feats), BF16),
        in_specs=[vmem_spec] * 3,
        out_specs=pl.BlockSpec(memory_space=pl.ANY),
        scratch_shapes=[pltpu.VMEM((tok_rows, feats), BF16), pltpu.SemaphoreType.DMA((tok_rows // 512,))],
        compiler_params=pltpu.CompilerParams(vmem_limit_bytes=60 * 2**20),
        cost_estimate=pl.CostEstimate(
            flops=2 * tok_rows * rows * feats, bytes_accessed=6 * 2**20, transcendentals=0
        ),
        name="mix",
    )(high, low, back)


def shards(tokens, router_weight, gate_weight, up_weight, down_weight, picks):
    tok_rows = tokens.shape[0]
    flight, capacity = picks.shape
    args = (tokens, router_weight, gate_weight, up_weight, down_weight)
    back, high, low, fit = route(*args, picks, True)

    def any_picks():
        blocks = picks.reshape(flight, DP, ROWS).transpose(1, 0, 2).reshape(DP, BLK)
        back, high, low, _ = route(*args, blocks, False)
        return mix(back, high, low, tok_rows)

    return lax.cond(fit[0, 0] <= NEAR, lambda: mix(back, high, low, tok_rows), any_picks)


def solution(mesh):
    in_specs = (
        P("dp", "group"),
        P("group", None),
        P("group", None, "dp"),
        P("group", None, "dp"),
        P("group", "dp", None),
        P(),
    )
    out_specs = P("dp", "group")
    return jax.shard_map(shards, mesh=mesh, in_specs=in_specs, out_specs=out_specs, check_vma=False)
```
